32 devices in a mesh: grid: 8 (over y, x, core), pts: 4 (over z).
Axes of the slice: x: 2, y: 2, z: 4, core: 2. Of those that a mesh axis runs over, the one named last changes fastest.
Arguments:
- orbitals: bfloat16 [512, 16384], P(None, 'grid'), may hold values from -0.8984375 to 0.8984375
- point_index: int32 [8192], P('pts'), may hold values from 0 to 16383
Outputs:
- screened: float32 [4, 2048, 128, 128], P('pts', 'grid')
The draws below stay inside these ranges and needn't reach their ends.
All inputs are finite; a program needn't handle non-finite values.
Results may differ from the reference program's by a relative error of at most 0.0003.
Values may be sent and summed in bfloat16 or wider, within the bound.
No kernel may reach another device: no remote copies, remote signals or barrier semaphores. Data moves between devices by JAX's collectives and lax.ppermute only.
A program may use at most 128 MiB of HBM per device.

```python
import jax
import jax.numpy as jnp
from jax import lax

SIDE = 128
NORB = 512
NPTS = 8192
NG = 16384
N_PTS = 4


def set_ends(array, key, low, top_value):
    dims = array.shape
    index_at = [jax.random.randint(jax.random.fold_in(key, axis), (), 0, dims[axis]) for axis in range(len(dims))]
    array = array.at[tuple(index_at)].set(low)
    longest = dims.index(max(dims))
    index_at[longest] = (index_at[longest] + 1) % dims[longest]
    return array.at[tuple(index_at)].set(top_value)


def levels(own_key, extent, shards, least, largest):
    def one(axis_at, shards_of):
        draws = jax.random.uniform(jax.random.fold_in(jax.random.fold_in(own_key, 6), axis_at), (shards_of,), jnp.float32, least / len(shards), largest / len(shards))
        return jnp.repeat(jnp.exp(draws), extent[axis_at] // shards_of).reshape((-1,) + (1,) * (len(extent) - axis_at - 1))

    gain = one(*shards[0])
    for cut in shards[1:]:
        gain = gain * one(*cut)
    return gain


def scatter_about(stream_key, shape, width, reach, pieces=(), held_as=jnp.bfloat16):
    entries = width * jax.random.normal(stream_key, shape, jnp.float32)
    if pieces:
        entries = entries * levels(stream_key, shape, pieces, -0.22, 0.18)
    return jnp.clip(entries, -reach, reach).astype(held_as)


def setup_inputs(seed: int = 0) -> dict:
    key_of = jax.random.split(jax.random.key(seed), 3)
    return {
        "orbitals": scatter_about(key_of[0], (NORB, NG), 0.15, 0.8984375, ((1, 8),)),
        "point_index": set_ends(jax.random.randint(key_of[1], (NPTS,), 0, NG), jax.random.fold_in(key_of[1], 1), 0, NG - 1).astype(jnp.int32),
    }


def screen_kernel():
    frequency = jnp.arange(SIDE, dtype=jnp.int32)
    wavenumber = jnp.minimum(frequency, SIDE - frequency).astype(jnp.float32)
    screening = SIDE / 16.0
    values = screening / jnp.sqrt(wavenumber[:, None] ** 2 + wavenumber[None, :] ** 2 + screening * screening)
    anchor = (frequency[:, None] == 0) & (frequency[None, :] == 0)
    return jnp.where(anchor, jnp.zeros_like(values), values)

def reference(orbitals, point_index):
    picked = jnp.take(orbitals, point_index, axis=1)
    kernel_values = screen_kernel()
    block_points = min(256, NPTS)
    chosen_blocks = picked.reshape(NORB, NPTS // block_points, block_points).transpose(1, 0, 2)

    def one_block(chosen_rows):
        pair_values = jnp.dot(chosen_rows.T, orbitals, preferred_element_type=jnp.float32)
        squared = (pair_values * pair_values).reshape(block_points, SIDE, SIDE)
        spectrum = jnp.fft.fft2(squared) * kernel_values
        return jnp.real(jnp.fft.ifft2(spectrum)).astype(jnp.float32)
    result = lax.map(one_block, chosen_blocks)
    return result.reshape(N_PTS, NPTS // N_PTS, SIDE, SIDE)
```

```python
import functools
import math

import jax
import jax.numpy as jnp
import numpy as np
from jax import lax
from jax.experimental import pallas as pl
from jax.experimental.pallas import tpu as pltpu
from jax.sharding import PartitionSpec as P

SIDE = 128
VMEM_BYTES = 60 * 2**20


def rotate(value, turn):
    re, im = value
    turn = turn % 1.0
    if turn == 0.0:
        return (re, im)
    if turn == 0.25:
        return (-im, re)
    if turn == 0.5:
        return (-re, -im)
    if turn == 0.75:
        return (im, -re)
    cos, sin = math.cos(2 * math.pi * turn), math.sin(2 * math.pi * turn)
    if turn in (0.125, 0.375, 0.625, 0.875):
        plus, minus = (re + im) * abs(cos), (re - im) * abs(cos)
        if turn == 0.125:
            return (minus, plus)
        if turn == 0.375:
            return (-plus, minus)
        if turn == 0.625:
            return (-minus, -plus)
        return (plus, -minus)
    return (re * cos - im * sin, re * sin + im * cos)


def add(a, b):
    return (a[0] + b[0], a[1] + b[1])


def sub(a, b):
    return (a[0] - b[0], a[1] - b[1])


def complex_dft(values, sign):
    n = len(values)
    if n == 1:
        return list(values)
    if n == 2:
        return [add(values[0], values[1]), sub(values[0], values[1])]
    if n % 4 == 0:
        parts = [complex_dft(values[r::4], sign) for r in range(4)]
        out = [None] * n
        quarter = n // 4
        for k in range(quarter):
            t0, t1, t2, t3 = (rotate(parts[r][k], sign * r * k / n) for r in range(4))
            s02, d02 = add(t0, t2), sub(t0, t2)
            s13, d13 = add(t1, t3), sub(t1, t3)
            out[k] = add(s02, s13)
            out[k + 2 * quarter] = sub(s02, s13)
            if sign < 0:
                out[k + quarter] = (d02[0] + d13[1], d02[1] - d13[0])
                out[k + 3 * quarter] = (d02[0] - d13[1], d02[1] + d13[0])
            else:
                out[k + quarter] = (d02[0] - d13[1], d02[1] + d13[0])
                out[k + 3 * quarter] = (d02[0] + d13[1], d02[1] - d13[0])
        return out
    even, odd = complex_dft(values[0::2], sign), complex_dft(values[1::2], sign)
    turned = [rotate(odd[k], sign * k / n) for k in range(n // 2)]
    return [add(even[k], turned[k]) for k in range(n // 2)] + [
        sub(even[k], turned[k]) for k in range(n // 2)
    ]


def real_dft(values):
    n = len(values)
    if n == 1:
        return [values[0]]
    if n == 2:
        return [values[0] + values[1], values[0] - values[1]]
    even, odd = real_dft(values[0::2]), real_dft(values[1::2])
    out = [None] * (n // 2 + 1)
    out[0], out[n // 2] = even[0] + odd[0], even[0] - odd[0]
    for k in range(1, n // 4):
        turned = rotate(odd[k], -k / n)
        low, high = add(even[k], turned), sub(even[k], turned)
        out[k], out[n // 2 - k] = low, (high[0], -high[1])
    out[n // 4] = (even[n // 4], -odd[n // 4])
    return out


def real_inverse(entries):
    n = 2 * (len(entries) - 1)
    if n == 2:
        return [entries[0] + entries[1], entries[0] - entries[1]]
    even, odd = [None] * (n // 4 + 1), [None] * (n // 4 + 1)
    even[0], odd[0] = entries[0] + entries[n // 2], entries[0] - entries[n // 2]
    for k in range(1, n // 4):
        other = entries[n // 2 - k]
        other = (other[0], -other[1])
        even[k] = add(entries[k], other)
        odd[k] = rotate(sub(entries[k], other), k / n)
    middle = entries[n // 4]
    even[n // 4], odd[n // 4] = 2.0 * middle[0], -2.0 * middle[1]
    out = [None] * n
    out[0::2], out[1::2] = real_inverse(even), real_inverse(odd)
    return out


def circulant_tables():
    frequency = np.arange(SIDE)
    wavenumber = np.minimum(frequency, SIDE - frequency).astype(np.float64)
    screening = SIDE / 16.0
    values = screening / np.sqrt(
        wavenumber[:, None] ** 2 + wavenumber[None, :] ** 2 + screening * screening
    )
    values[0, 0] = 0.0
    cosines = np.cos(2 * np.pi * np.outer(frequency, frequency) / SIDE)
    taps = values[: SIDE // 2 + 1] @ cosines / (SIDE * SIDE)
    shift = (frequency[None, :] - frequency[:, None]) % SIDE
    tables = taps[:, shift].astype(np.float32)
    high = tables.astype(jnp.bfloat16)
    low = (tables - high.astype(np.float32)).astype(jnp.bfloat16)
    return jnp.asarray(np.concatenate([high, low], axis=2))


def pick_kernel(index_ref, orbitals_ref, out_ref):
    points, cells = index_ref.shape[0], orbitals_ref.shape[1]
    hot = lax.broadcasted_iota(jnp.int32, (points, cells), 1) == index_ref[...]
    hot = jnp.where(hot, 1.0, 0.0).astype(jnp.bfloat16)
    out_ref[...] = lax.dot_general(
        hot, orbitals_ref[...], (((1,), (1,)), ((), ())), preferred_element_type=jnp.float32
    ).astype(jnp.bfloat16)


def pick_own(local_index, orbitals):
    points, (orbital_count, cells) = local_index.shape[0], orbitals.shape
    block = min(256, points)
    return pl.pallas_call(
        pick_kernel,
        grid=(points // block,),
        in_specs=[
            pl.BlockSpec((block, 1), lambda i: (i, 0)),
            pl.BlockSpec((orbital_count, cells), lambda i: (0, 0)),
        ],
        out_specs=pl.BlockSpec((block, orbital_count), lambda i: (i, 0)),
        out_shape=jax.ShapeDtypeStruct((points, orbital_count), jnp.bfloat16),
        compiler_params=pltpu.CompilerParams(vmem_limit_bytes=VMEM_BYTES),
        cost_estimate=pl.CostEstimate(
            flops=2 * points * orbital_count * cells,
            bytes_accessed=2 * orbital_count * (cells + points),
            transcendentals=0,
        ),
    )(local_index[:, None], orbitals)


def sheet_kernel(layout, picked_ref, tables_ref, *refs):
    count, parts_of = layout
    arrays = refs[: -7]
    out_ref, cells_ref, squared_ref, slots_ref, stage_ref, in_sem, out_sem = refs[-7:]
    rows = SIDE // count
    points = picked_ref.shape[0]
    half = count // 2
    pair_rows = 2
    steps = rows // pair_rows
    me = lax.axis_index("grid")

    def fetch(step, slot):
        return [
            pltpu.make_async_copy(
                arrays[which].at[:, pl.ds(step * pair_rows * SIDE, pair_rows * SIDE)],
                cells_ref.at[slot, apart, pl.ds(first, size), :],
                in_sem.at[slot],
            )
            for apart, parts in enumerate(parts_of)
            for which, first, size in parts
        ]

    for copy in fetch(0, 0):
        copy.start()
    for step in range(steps):
        slot = step % 2
        if step + 1 < steps:
            for copy in fetch(step + 1, 1 - slot):
                copy.start()
        for copy in fetch(step, slot):
            copy.wait()

        def multiply(apart, carry):
            pair = jnp.dot(
                picked_ref[...], cells_ref[slot, apart], preferred_element_type=jnp.float32
            )
            squared_ref[me ^ apart] = pair * pair
            return carry

        lax.fori_loop(0, count, multiply, 0)
        chunk = 8

        def spread(at, carry):
            here = pl.ds(pl.multiple_of(at * chunk, chunk), chunk)
            for within in range(pair_rows):
                j = step * pair_rows + within
                lanes = pl.ds(within * SIDE, SIDE)
                entries = real_dft([squared_ref[g, here, lanes] for g in range(count)])
                slots_ref[0, j, here, :] = entries[0]
                slots_ref[count - 1, j, here, :] = entries[half]
                for k in range(1, half):
                    re, im = rotate(entries[k], -k * j / SIDE)
                    slots_ref[2 * k - 1, j, here, :] = re
                    slots_ref[2 * k, j, here, :] = im
            return carry

        lax.fori_loop(0, points // chunk, spread, 0, unroll=2)

    def circulant(blocks, a):
        stacked = blocks[0] if len(blocks) == 1 else jnp.concatenate(blocks, axis=0)
        high = stacked.astype(jnp.bfloat16)
        low = (stacked - high.astype(jnp.float32)).astype(jnp.bfloat16)
        table = tables_ref[min(a, SIDE - a)]
        both = jnp.dot(
            jnp.concatenate([high, low], axis=1),
            jnp.concatenate([table, table], axis=0),
            preferred_element_type=jnp.float32,
        )
        return both[:, :SIDE] + both[:, SIDE:]

    chunk = 8

    def over_points(body):
        def one(at, carry):
            body(pl.ds(pl.multiple_of(at * chunk, chunk), chunk))
            return carry

        lax.fori_loop(0, points // chunk, one, 0)

    def apply(places, a):
        outs = circulant([slots_ref[s, j] for s, j in places], a)
        for at, (s, j) in enumerate(places):
            slots_ref[s, j] = outs[at * points : (at + 1) * points]

    def real_there(here):
        entries = real_dft([slots_ref[0, j, here, :] for j in range(rows)])
        slots_ref[0, 0, here, :] = entries[0]
        slots_ref[0, rows - 1, here, :] = entries[rows // 2]
        for k in range(1, rows // 2):
            slots_ref[0, 2 * k - 1, here, :], slots_ref[0, 2 * k, here, :] = entries[k]

    def real_back(here):
        entries = [slots_ref[0, 0, here, :]]
        for k in range(1, rows // 2):
            entries.append((slots_ref[0, 2 * k - 1, here, :], slots_ref[0, 2 * k, here, :]))
        entries.append(slots_ref[0, rows - 1, here, :])
        for j, value in enumerate(real_inverse(entries)):
            slots_ref[0, j, here, :] = value

    over_points(real_there)
    apply([(0, 0)], 0)
    apply([(0, rows - 1)], SIDE // 2)
    for k in range(1, rows // 2):
        apply([(0, 2 * k - 1), (0, 2 * k)], count * k)
    over_points(real_back)

    last = count - 1
    short = rows // 2

    def odd_there(here):
        values = [
            rotate((slots_ref[last, j, here, :], -slots_ref[last, j + short, here, :]), -j / (2 * rows))
            for j in range(short)
        ]
        for k, (re, im) in enumerate(complex_dft(values, -1)):
            slots_ref[last, 2 * k, here, :] = re
            slots_ref[last, 2 * k + 1, here, :] = im

    def odd_back(here):
        values = [
            (slots_ref[last, 2 * k, here, :], slots_ref[last, 2 * k + 1, here, :])
            for k in range(short)
        ]
        for j, value in enumerate(complex_dft(values, 1)):
            re, im = rotate(value, j / (2 * rows))
            slots_ref[last, j, here, :] = 2.0 * re
            slots_ref[last, j + short, here, :] = -2.0 * im

    over_points(odd_there)
    for k in range(short):
        apply([(last, 2 * k), (last, 2 * k + 1)], half + 2 * count * k)
    over_points(odd_back)

    for k in range(1, half):
        re_slot, im_slot = 2 * k - 1, 2 * k

        def complex_there(here, sign=-1):
            values = [
                (slots_ref[re_slot, j, here, :], slots_ref[im_slot, j, here, :])
                for j in range(rows)
            ]
            for j, (re, im) in enumerate(complex_dft(values, sign)):
                slots_ref[re_slot, j, here, :] = re
                slots_ref[im_slot, j, here, :] = im

        over_points(complex_there)
        for a2 in range(rows):
            apply([(re_slot, a2), (im_slot, a2)], k + count * a2)
        over_points(functools.partial(complex_there, sign=1))

    def put(j, slot):
        return [
            pltpu.make_async_copy(
                stage_ref.at[slot, g], out_ref.at[:, rows * g + j, :], out_sem.at[slot]
            )
            for g in range(count)
        ]

    for j in range(rows):
        slot = j % 2
        if j >= 2:
            for copy in put(j - 2, slot):
                copy.wait()

        def gather_back(here):
            entries = [slots_ref[0, j, here, :]]
            for k in range(1, half):
                entries.append(
                    rotate(
                        (slots_ref[2 * k - 1, j, here, :], slots_ref[2 * k, j, here, :]),
                        k * j / SIDE,
                    )
                )
            entries.append(slots_ref[count - 1, j, here, :])
            for g, value in enumerate(real_inverse(entries)):
                stage_ref[slot, g, here, :] = value

        over_points(gather_back)
        for copy in put(j, slot):
            copy.start()
    for j in range(max(rows - 2, 0), rows):
        for copy in put(j, j % 2):
            copy.wait()


def screen_sheets(picked, tables, shard_parts, count):
    points, orbital_count = picked.shape
    arrays, parts_of = [], []
    for parts in shard_parts:
        entry = []
        for array, first in parts:
            entry.append((len(arrays), first, array.shape[0]))
            arrays.append(array)
        parts_of.append(tuple(entry))
    rows = SIDE // count
    vmem = pl.BlockSpec(memory_space=pltpu.VMEM)
    return pl.pallas_call(
        functools.partial(sheet_kernel, (count, tuple(parts_of))),
        in_specs=[vmem, vmem] + [pl.BlockSpec(memory_space=pl.ANY)] * len(arrays),
        out_specs=pl.BlockSpec(memory_space=pl.ANY),
        out_shape=jax.ShapeDtypeStruct((points, SIDE, SIDE), jnp.float32),
        scratch_shapes=[
            pltpu.VMEM((2, count, orbital_count, 2 * SIDE), jnp.bfloat16),
            pltpu.VMEM((count, points, 2 * SIDE), jnp.float32),
            pltpu.VMEM((count, rows, points, SIDE), jnp.float32),
            pltpu.VMEM((2, count, points, SIDE), jnp.float32),
            pltpu.SemaphoreType.DMA((2,)),
            pltpu.SemaphoreType.DMA((2,)),
        ],
        compiler_params=pltpu.CompilerParams(vmem_limit_bytes=VMEM_BYTES),
        cost_estimate=pl.CostEstimate(
            flops=2 * points * orbital_count * SIDE * SIDE,
            bytes_accessed=points * SIDE * SIDE * 8,
            transcendentals=0,
        ),
    )(picked, tables, *arrays)


def swap(array, mask):
    count = lax.axis_size("grid")
    return lax.ppermute(array, "grid", [(i, i ^ mask) for i in range(count)])


def scatter_points(own, masks):
    count = lax.axis_size("grid")
    bits = count.bit_length() - 1
    me = lax.axis_index("grid")
    value = own.reshape((2,) * bits + (own.shape[0] // count, own.shape[1]))
    left = list(range(bits))[::-1]
    for bit in masks:
        axis = left.index(bit)
        mine = (me >> bit) & 1
        keep = lax.dynamic_index_in_dim(value, mine, axis, keepdims=False)
        send = lax.dynamic_index_in_dim(value, 1 - mine, axis, keepdims=False)
        value = keep + swap(send, 1 << bit)
        left.remove(bit)
    return value


def gather_cells(orbitals):
    count = lax.axis_size("grid")
    bits = count.bit_length() - 1
    middle = orbitals.shape[0] // 2
    held = {0: [(orbitals, 0)]}
    link_bits = list(range(1, bits))
    cut = (len(link_bits) + 1) // 2
    routes = (link_bits, link_bits[cut:] + link_bits[:cut])
    pieces = ({0: orbitals[:middle]}, {0: orbitals[middle:]})
    for hop in range(len(link_bits)):
        for route, have in zip(routes, pieces):
            mask = 1 << route[hop]
            for known in sorted(have):
                have[known | mask] = swap(have[known], mask)
    for known in pieces[0]:
        if known:
            held[known] = [(pieces[0][known], 0), (pieces[1][known], middle)]
    for known in sorted(held):
        held[known | 1] = [(swap(array, 1), first) for array, first in held[known]]
    return [held[d] for d in range(count)]


def shards(orbitals, point_index):
    cell_count = orbitals.shape[1]
    count = lax.axis_size("grid")
    bits = count.bit_length() - 1
    local_index = point_index - lax.axis_index("grid") * cell_count
    shard_parts = gather_cells(orbitals)
    own = pick_own(local_index, orbitals)
    picked = scatter_points(own, list(range(bits)))
    return screen_sheets(picked, circulant_tables(), shard_parts, count)[None]


def solution(mesh):
    in_specs = (P(None, "grid"), P("pts"))
    out_specs = P("pts", "grid", None, None)
    return jax.shard_map(shards, mesh=mesh, in_specs=in_specs, out_specs=out_specs, check_vma=False)
```

```python
import functools
import math

import jax
import jax.numpy as jnp
import numpy as np
from jax import lax
from jax.experimental import pallas as pl
from jax.experimental.pallas import tpu as pltpu
from jax.sharding import PartitionSpec as P

SIDE = 128
VMEM_BYTES = 60 * 2**20
STAGES = 4


def rotate(value, turn):
    re, im = value
    turn = turn % 1.0
    if turn == 0.0:
        return (re, im)
    if turn == 0.25:
        return (-im, re)
    if turn == 0.5:
        return (-re, -im)
    if turn == 0.75:
        return (im, -re)
    cos, sin = math.cos(2 * math.pi * turn), math.sin(2 * math.pi * turn)
    if turn in (0.125, 0.375, 0.625, 0.875):
        plus, minus = (re + im) * abs(cos), (re - im) * abs(cos)
        if turn == 0.125:
            return (minus, plus)
        if turn == 0.375:
            return (-plus, minus)
        if turn == 0.625:
            return (-minus, -plus)
        return (plus, -minus)
    return (re * cos - im * sin, re * sin + im * cos)


def add(a, b):
    return (a[0] + b[0], a[1] + b[1])


def sub(a, b):
    return (a[0] - b[0], a[1] - b[1])


def complex_dft(values, sign):
    n = len(values)
    if n == 1:
        return list(values)
    if n == 2:
        return [add(values[0], values[1]), sub(values[0], values[1])]
    if n % 4 == 0:
        parts = [complex_dft(values[r::4], sign) for r in range(4)]
        out = [None] * n
        quarter = n // 4
        for k in range(quarter):
            t0, t1, t2, t3 = (rotate(parts[r][k], sign * r * k / n) for r in range(4))
            s02, d02 = add(t0, t2), sub(t0, t2)
            s13, d13 = add(t1, t3), sub(t1, t3)
            out[k] = add(s02, s13)
            out[k + 2 * quarter] = sub(s02, s13)
            if sign < 0:
                out[k + quarter] = (d02[0] + d13[1], d02[1] - d13[0])
                out[k + 3 * quarter] = (d02[0] - d13[1], d02[1] + d13[0])
            else:
                out[k + quarter] = (d02[0] - d13[1], d02[1] + d13[0])
                out[k + 3 * quarter] = (d02[0] + d13[1], d02[1] - d13[0])
        return out
    even, odd = complex_dft(values[0::2], sign), complex_dft(values[1::2], sign)
    turned = [rotate(odd[k], sign * k / n) for k in range(n // 2)]
    return [add(even[k], turned[k]) for k in range(n // 2)] + [
        sub(even[k], turned[k]) for k in range(n // 2)
    ]


def real_dft(values):
    n = len(values)
    if n == 1:
        return [values[0]]
    if n == 2:
        return [values[0] + values[1], values[0] - values[1]]
    even, odd = real_dft(values[0::2]), real_dft(values[1::2])
    out = [None] * (n // 2 + 1)
    out[0], out[n // 2] = even[0] + odd[0], even[0] - odd[0]
    for k in range(1, n // 4):
        turned = rotate(odd[k], -k / n)
        low, high = add(even[k], turned), sub(even[k], turned)
        out[k], out[n // 2 - k] = low, (high[0], -high[1])
    out[n // 4] = (even[n // 4], -odd[n // 4])
    return out


def real_inverse(entries):
    n = 2 * (len(entries) - 1)
    if n == 2:
        return [entries[0] + entries[1], entries[0] - entries[1]]
    even, odd = [None] * (n // 4 + 1), [None] * (n // 4 + 1)
    even[0], odd[0] = entries[0] + entries[n // 2], entries[0] - entries[n // 2]
    for k in range(1, n // 4):
        other = entries[n // 2 - k]
        other = (other[0], -other[1])
        even[k] = add(entries[k], other)
        odd[k] = rotate(sub(entries[k], other), k / n)
    middle = entries[n // 4]
    even[n // 4], odd[n // 4] = 2.0 * middle[0], -2.0 * middle[1]
    out = [None] * n
    out[0::2], out[1::2] = real_inverse(even), real_inverse(odd)
    return out


def circulant_tables():
    frequency = np.arange(SIDE)
    wavenumber = np.minimum(frequency, SIDE - frequency).astype(np.float64)
    screening = SIDE / 16.0
    values = screening / np.sqrt(
        wavenumber[:, None] ** 2 + wavenumber[None, :] ** 2 + screening * screening
    )
    values[0, 0] = 0.0
    cosines = np.cos(2 * np.pi * np.outer(frequency, frequency) / SIDE)
    taps = values[: SIDE // 2 + 1] @ cosines / (SIDE * SIDE)
    shift = (frequency[None, :] - frequency[:, None]) % SIDE
    tables = taps[:, shift].astype(np.float32)
    high = tables.astype(jnp.bfloat16)
    low = (tables - high.astype(np.float32)).astype(jnp.bfloat16)
    return jnp.asarray(np.concatenate([high, low], axis=2))


def fetches(step, slot, apart, arrays, cells_ref, in_sem):
    _, column, parts = step[2][apart]
    width = step[1] * SIDE
    return [
        pltpu.make_async_copy(
            arrays[which].at[:, pl.ds(column, width)],
            cells_ref.at[slot, apart, pl.ds(first, size), pl.ds(0, width)],
            in_sem.at[slot, apart],
        )
        for which, first, size in parts
    ]


def holder(step, apart):
    even_mask, odd_mask = step[2][apart][0]
    me, odd = lax.axis_index("grid"), lax.axis_index("pts") & 1
    if even_mask == odd_mask:
        return me ^ even_mask
    return me ^ (even_mask ^ (odd * (even_mask ^ odd_mask)))


def pick_from(step, apart, index_ref, cells):
    width, count = step[1] * SIDE, len(step[2])
    base = holder(step, apart) * (SIDE * SIDE // count) + step[0] * SIDE
    shape = (index_ref.shape[0], width)
    hot = lax.broadcasted_iota(jnp.int32, shape, 1) == index_ref[...] - base
    return lax.dot_general(
        jnp.where(hot, 1.0, 0.0).astype(jnp.bfloat16),
        cells,
        (((1,), (1,)), ((), ())),
        preferred_element_type=jnp.float32,
    )


def pick_kernel(steps, index_ref, *refs):
    *arrays, out_ref, cells_ref, total_ref, in_sem = refs
    count = len(steps[0][2])

    def start(at):
        for apart in range(count):
            for copy in fetches(steps[at], at % 2, apart, arrays, cells_ref, in_sem):
                copy.start()

    start(0)
    total_ref[...] = jnp.zeros_like(total_ref)
    for at, step in enumerate(steps):
        if at + 1 < len(steps):
            start(at + 1)
        for apart in range(count):
            for copy in fetches(step, at % 2, apart, arrays, cells_ref, in_sem):
                copy.wait()
            cells = cells_ref[at % 2, apart, :, : step[1] * SIDE]
            total_ref[...] += pick_from(step, apart, index_ref, cells)
    out_ref[...] = total_ref[...].astype(jnp.bfloat16)


def sheet_kernel(steps, pick_first, index_ref, picked_ref, far_tables_ref, *refs):
    *arrays, out_ref, chosen_ref, cells_ref, squared_ref, slots_ref, stage_ref = refs[:-4]
    tables_ref, in_sem, out_sem, table_sem = refs[-4:]
    table_copy = pltpu.make_async_copy(far_tables_ref, tables_ref, table_sem.at[0])
    count = len(steps[0][2])
    rows = SIDE // count
    points = picked_ref.shape[0]
    half = count // 2
    chunk = 8

    def start(at):
        for apart in range(count):
            for copy in fetches(steps[at], at % 2, apart, arrays, cells_ref, in_sem):
                copy.start()

    def wait(at, apart):
        for copy in fetches(steps[at], at % 2, apart, arrays, cells_ref, in_sem):
            copy.wait()

    for at in range(max(1, pick_first)):
        start(at)
    table_copy.start()
    if pick_first:
        total = picked_ref[...].astype(jnp.float32)
        for at in range(pick_first):
            for apart in range(count):
                wait(at, apart)
                cells = cells_ref[at, apart, :, : steps[at][1] * SIDE]
                total += pick_from(steps[at], apart, index_ref, cells)
        chosen_ref[...] = total.astype(jnp.bfloat16)
    else:
        chosen_ref[...] = picked_ref[...]

    for at, step in enumerate(steps):
        first_row, rows_here, _ = step
        width = rows_here * SIDE
        if max(1, pick_first) <= at + 1 < len(steps):
            start(at + 1)
        for apart in range(count):
            if at >= pick_first:
                wait(at, apart)
            pair = jnp.dot(
                chosen_ref[...],
                cells_ref[at % 2, apart, :, :width],
                preferred_element_type=jnp.float32,
            )
            squared_ref[holder(step, apart), :, :width] = pair * pair

        def spread(here, first_row=first_row, rows_here=rows_here):
            for within in range(rows_here):
                j = first_row + within
                lanes = pl.ds(within * SIDE, SIDE)
                entries = real_dft([squared_ref[g, here, lanes] for g in range(count)])
                slots_ref[0, j, here, :] = entries[0]
                slots_ref[count - 1, j, here, :] = entries[half]
                for k in range(1, half):
                    re, im = rotate(entries[k], -k * j / SIDE)
                    slots_ref[2 * k - 1, j, here, :] = re
                    slots_ref[2 * k, j, here, :] = im

        def one(at_chunk, carry):
            spread(pl.ds(pl.multiple_of(at_chunk * chunk, chunk), chunk))
            return carry

        lax.fori_loop(0, points // chunk, one, 0)

    table_copy.wait()

    def circulant(blocks, a):
        stacked = blocks[0] if len(blocks) == 1 else jnp.concatenate(blocks, axis=0)
        high = stacked.astype(jnp.bfloat16)
        low = (stacked - high.astype(jnp.float32)).astype(jnp.bfloat16)
        table = tables_ref[min(a, SIDE - a)]
        both = jnp.dot(
            jnp.concatenate([high, low], axis=1),
            jnp.concatenate([table, table], axis=0),
            preferred_element_type=jnp.float32,
        )
        return both[:, :SIDE] + both[:, SIDE:]

    def over_points(body, unroll):
        def one(at, carry):
            body(pl.ds(pl.multiple_of(at * chunk, chunk), chunk))
            return carry

        lax.fori_loop(0, points // chunk, one, 0, unroll=min(unroll, points // chunk))

    def apply(places, a):
        outs = circulant([slots_ref[s, j] for s, j in places], a)
        for at, (s, j) in enumerate(places):
            slots_ref[s, j] = outs[at * points : (at + 1) * points]

    def real_there(here):
        entries = real_dft([slots_ref[0, j, here, :] for j in range(rows)])
        slots_ref[0, 0, here, :] = entries[0]
        slots_ref[0, rows - 1, here, :] = entries[rows // 2]
        for k in range(1, rows // 2):
            slots_ref[0, 2 * k - 1, here, :], slots_ref[0, 2 * k, here, :] = entries[k]

    def real_back(here):
        entries = [slots_ref[0, 0, here, :]]
        for k in range(1, rows // 2):
            entries.append((slots_ref[0, 2 * k - 1, here, :], slots_ref[0, 2 * k, here, :]))
        entries.append(slots_ref[0, rows - 1, here, :])
        for j, value in enumerate(real_inverse(entries)):
            slots_ref[0, j, here, :] = value

    over_points(real_there, 4)
    apply([(0, 0)], 0)
    apply([(0, rows - 1)], SIDE // 2)
    for k in range(1, rows // 2):
        apply([(0, 2 * k - 1), (0, 2 * k)], count * k)
    over_points(real_back, 4)

    last = count - 1
    short = rows // 2

    def odd_there(here):
        values = [
            rotate((slots_ref[last, j, here, :], -slots_ref[last, j + short, here, :]), -j / (2 * rows))
            for j in range(short)
        ]
        for k, (re, im) in enumerate(complex_dft(values, -1)):
            slots_ref[last, 2 * k, here, :] = re
            slots_ref[last, 2 * k + 1, here, :] = im

    def odd_back(here):
        values = [
            (slots_ref[last, 2 * k, here, :], slots_ref[last, 2 * k + 1, here, :])
            for k in range(short)
        ]
        for j, value in enumerate(complex_dft(values, 1)):
            re, im = rotate(value, j / (2 * rows))
            slots_ref[last, j, here, :] = 2.0 * re
            slots_ref[last, j + short, here, :] = -2.0 * im

    over_points(odd_there, 4)
    for k in range(short):
        apply([(last, 2 * k), (last, 2 * k + 1)], half + 2 * count * k)
    over_points(odd_back, 4)

    for k in range(1, half):
        re_slot, im_slot = 2 * k - 1, 2 * k

        def complex_there(here, sign=-1):
            values = [
                (slots_ref[re_slot, j, here, :], slots_ref[im_slot, j, here, :])
                for j in range(rows)
            ]
            for j, (re, im) in enumerate(complex_dft(values, sign)):
                slots_ref[re_slot, j, here, :] = re
                slots_ref[im_slot, j, here, :] = im

        over_points(complex_there, 4)
        for a2 in range(rows):
            apply([(re_slot, a2), (im_slot, a2)], k + count * a2)
        over_points(functools.partial(complex_there, sign=1), 4)

    def put(j, slot):
        return [
            pltpu.make_async_copy(
                stage_ref.at[slot, g], out_ref.at[:, rows * g + j, :], out_sem.at[slot]
            )
            for g in range(count)
        ]

    for j in range(rows):
        slot = j % STAGES
        if j >= STAGES:
            for copy in put(j - STAGES, slot):
                copy.wait()

        def gather_back(here):
            entries = [slots_ref[0, j, here, :]]
            for k in range(1, half):
                entries.append(
                    rotate(
                        (slots_ref[2 * k - 1, j, here, :], slots_ref[2 * k, j, here, :]),
                        k * j / SIDE,
                    )
                )
            entries.append(slots_ref[count - 1, j, here, :])
            for g, value in enumerate(real_inverse(entries)):
                stage_ref[slot, g, here, :] = value

        over_points(gather_back, 4)
        for copy in put(j, slot):
            copy.start()
    for j in range(max(rows - STAGES, 0), rows):
        for copy in put(j, j % STAGES):
            copy.wait()


VMEM_SPEC = pl.BlockSpec(memory_space=pltpu.VMEM)
ANY_SPEC = pl.BlockSpec(memory_space=pl.ANY)


def flatten(steps):
    arrays, plan = [], []
    for first_row, rows_here, entries in steps:
        numbered = []
        for masks, column, parts in entries:
            for array, _ in parts:
                if not any(array is known for known in arrays):
                    arrays.append(array)
            which = [next(i for i, known in enumerate(arrays) if known is array) for array, _ in parts]
            numbered.append(
                (masks, column, tuple((w, first, a.shape[0]) for w, (a, first) in zip(which, parts)))
            )
        plan.append((first_row, rows_here, tuple(numbered)))
    return tuple(plan), arrays


def cell_buffers(plan, orbital_count):
    widest = max(rows_here for _, rows_here, _ in plan) * SIDE
    return pltpu.VMEM((min(2, len(plan)), len(plan[0][2]), orbital_count, widest), jnp.bfloat16)


def pick_cells(index, orbital_count, steps, us=0):
    plan, arrays = flatten(steps)
    count = len(plan[0][2])
    shape = (index.shape[0], orbital_count)
    return pl.pallas_call(
        functools.partial(pick_kernel, plan),
        in_specs=[VMEM_SPEC] + [ANY_SPEC] * len(arrays),
        out_specs=VMEM_SPEC,
        out_shape=jax.ShapeDtypeStruct(shape, jnp.bfloat16),
        scratch_shapes=[
            cell_buffers(plan, orbital_count),
            pltpu.VMEM(shape, jnp.float32),
            pltpu.SemaphoreType.DMA((2, count)),
        ],
        compiler_params=pltpu.CompilerParams(vmem_limit_bytes=VMEM_BYTES),
        cost_estimate=pl.CostEstimate(flops=us * 5 * 10**8, bytes_accessed=0, transcendentals=0),
    )(index, *arrays)


def screen_sheets(index, picked, tables, steps, pick_first):
    points, orbital_count = picked.shape
    plan, arrays = flatten(steps)
    count = len(plan[0][2])
    rows = SIDE // count
    widest = max(rows_here for _, rows_here, _ in plan) * SIDE
    return pl.pallas_call(
        functools.partial(sheet_kernel, plan, pick_first),
        in_specs=[VMEM_SPEC] * 2 + [ANY_SPEC] * (1 + len(arrays)),
        out_specs=ANY_SPEC,
        out_shape=jax.ShapeDtypeStruct((points, SIDE, SIDE), jnp.float32),
        scratch_shapes=[
            pltpu.VMEM((points, orbital_count), jnp.bfloat16),
            cell_buffers(plan, orbital_count),
            pltpu.VMEM((count, points, widest), jnp.float32),
            pltpu.VMEM((count, rows, points, SIDE), jnp.float32),
            pltpu.VMEM((STAGES, count, points, SIDE), jnp.float32),
            pltpu.VMEM(tables.shape, tables.dtype),
            pltpu.SemaphoreType.DMA((2, count)),
            pltpu.SemaphoreType.DMA((STAGES,)),
            pltpu.SemaphoreType.DMA((1,)),
        ],
        compiler_params=pltpu.CompilerParams(vmem_limit_bytes=VMEM_BYTES),
    )(index, picked, tables, *arrays)


def swap(array, mask):
    count = lax.axis_size("grid")
    return lax.ppermute(array, "grid", [(i, i ^ mask) for i in range(count)])


def routes(bits):
    cut = (bits - 1) // 2
    links = list(range(1, bits))
    return links, links[cut:] + links[:cut]


class Order:
    def __init__(self, seed):
        self.token = seed

    def start(self, move, array, *arguments):
        array, _ = lax.optimization_barrier((array, self.token))
        return move(array, *arguments)

    def wait(self, *arrays):
        self.token, *_ = lax.optimization_barrier((self.token, *arrays))


def gather_cells(orbitals):
    count = lax.axis_size("grid")
    bits = count.bit_length() - 1
    middle = orbitals.shape[0] // 2
    held = {0: [(orbitals, 0)]}
    pieces = ({0: orbitals[:middle]}, {0: orbitals[middle:]})
    for route, have in zip(routes(bits), pieces):
        for bit in route:
            for known in sorted(have):
                have[known | 1 << bit] = swap(have[known], 1 << bit)
    for known in pieces[0]:
        if known:
            held[known] = [(pieces[0][known], 0), (pieces[1][known], middle)]
    for known in sorted(held):
        held[known | 1] = [(swap(array, 1), first) for array, first in held[known]]
    rows = SIDE // count
    return [
        (j, 1, [((d, d), j * SIDE, held[d]) for d in range(count)]) for j in range(rows)
    ]


CORE, NEAR, FAR = 1, 2, 4
SCRIPT = ("F0", "F1", "B", "P0", "F2", "P1", "F3", "S0", "P2", "S1", "W", "X3", "V2", "P3", "S2", "K012:0", "S3")
PIECE_ROWS = (4, 4, 4, 4)


def exchange(array, masks, across):
    count, planes = lax.axis_size("grid"), lax.axis_size("pts")
    pairs = [
        (g * planes + z, (g ^ masks[z & 1]) * planes + (z ^ across))
        for g in range(count)
        for z in range(planes)
    ]
    return lax.ppermute(array, ("grid", "pts"), pairs)


def four_chips(orbitals, index, tables):
    order = Order(index[:1])
    ends = [sum(PIECE_ROWS[:p]) for p in range(len(PIECE_ROWS) + 1)]
    first, far, core = {}, {}, {}

    def send_first(p):
        source = lax.optimization_barrier((orbitals, order.token))[0]
        piece = source[:, ends[p] * SIDE : ends[p + 1] * SIDE]
        first[p] = exchange(piece, (NEAR, FAR), 0)

    def pass_on(p):
        order.wait(first[p])
        far[p] = (
            order.start(exchange, first[p], (FAR, NEAR), 0),
            order.start(exchange, first[p], (0, 0), 1),
        )
        core[p] = [order.start(swap, first[p], CORE)]

    def share(p):
        order.wait(*far[p])
        core[p] += [order.start(swap, array, CORE) for array in far[p]]

    def step(p):
        order.wait(*core[p])
        entry = [
            ((0, 0), ends[p] * SIDE, [(orbitals, 0)]),
            ((CORE, CORE), ends[p] * SIDE, [(sibling, 0)]),
        ]
        arrays = (first[p], *far[p])
        for masks, array, other in zip(((NEAR, FAR), (NEAR | FAR,) * 2, (FAR, NEAR)), arrays, core[p]):
            entry.append((masks, 0, [(array, 0)]))
            entry.append((tuple(m | CORE for m in masks), 0, [(other, 0)]))
        return (ends[p], PIECE_ROWS[p], entry)

    steps, picks = {}, []
    for word in SCRIPT:
        op, arg = word[0], word[1:]
        if op == "F":
            send_first(int(arg))
        elif op == "P":
            pass_on(int(arg))
        elif op == "S":
            share(int(arg))
        elif op == "V":
            order.wait(*far[int(arg)])
        elif op == "X":
            order.wait(first[int(arg)])
        elif op == "B":
            sibling = order.start(swap, orbitals, CORE)
        elif op == "W":
            order.wait(sibling)
        elif op == "K":
            ids, cost = arg.split(":")
            for p in ids:
                steps[int(p)] = step(int(p))
            picks.append(pick_cells(index, orbitals.shape[0], [steps[int(p)] for p in ids], int(cost)))
            order.wait(picks[-1])
    left = [step(p) for p in range(len(PIECE_ROWS)) if p not in steps]
    picked = functools.reduce(lambda x, y: x + y, picks)
    return screen_sheets(index, picked, tables, left + [steps[p] for p in sorted(steps)], len(left))


def shards(orbitals, point_index):
    count = lax.axis_size("grid")
    points = point_index.shape[0] // count
    index = lax.dynamic_slice_in_dim(point_index, lax.axis_index("grid") * points, points)[:, None]
    tables = circulant_tables()
    if count == 8 and lax.axis_size("pts") % 2 == 0:
        return four_chips(orbitals, index, tables)[None]
    steps = gather_cells(orbitals)
    picked = pick_cells(index, orbitals.shape[0], steps)
    return screen_sheets(index, picked, tables, steps, 0)[None]


def solution(mesh):
    in_specs = (P(None, "grid"), P("pts"))
    out_specs = P("pts", "grid", None, None)
    return jax.shard_map(shards, mesh=mesh, in_specs=in_specs, out_specs=out_specs, check_vma=False)
```

```python
import functools
import math

import jax
import jax.numpy as jnp
import numpy as np
from jax import lax
from jax.experimental import pallas as pl
from jax.experimental.pallas import tpu as pltpu
from jax.sharding import PartitionSpec as P

SIDE = 128
VMEM_BYTES = 63 * 2**20
STAGES = 4


def rotate(value, turn):
    re, im = value
    turn = turn % 1.0
    if turn == 0.0:
        return (re, im)
    if turn == 0.25:
        return (-im, re)
    if turn == 0.5:
        return (-re, -im)
    if turn == 0.75:
        return (im, -re)
    cos, sin = math.cos(2 * math.pi * turn), math.sin(2 * math.pi * turn)
    if turn in (0.125, 0.375, 0.625, 0.875):
        plus, minus = (re + im) * abs(cos), (re - im) * abs(cos)
        if turn == 0.125:
            return (minus, plus)
        if turn == 0.375:
            return (-plus, minus)
        if turn == 0.625:
            return (-minus, -plus)
        return (plus, -minus)
    return (re * cos - im * sin, re * sin + im * cos)


def add(a, b):
    return (a[0] + b[0], a[1] + b[1])


def sub(a, b):
    return (a[0] - b[0], a[1] - b[1])


def complex_dft(values, sign):
    n = len(values)
    if n == 1:
        return list(values)
    if n == 2:
        return [add(values[0], values[1]), sub(values[0], values[1])]
    if n % 4 == 0:
        parts = [complex_dft(values[r::4], sign) for r in range(4)]
        out = [None] * n
        quarter = n // 4
        for k in range(quarter):
            t0, t1, t2, t3 = (rotate(parts[r][k], sign * r * k / n) for r in range(4))
            s02, d02 = add(t0, t2), sub(t0, t2)
            s13, d13 = add(t1, t3), sub(t1, t3)
            out[k] = add(s02, s13)
            out[k + 2 * quarter] = sub(s02, s13)
            if sign < 0:
                out[k + quarter] = (d02[0] + d13[1], d02[1] - d13[0])
                out[k + 3 * quarter] = (d02[0] - d13[1], d02[1] + d13[0])
            else:
                out[k + quarter] = (d02[0] - d13[1], d02[1] + d13[0])
                out[k + 3 * quarter] = (d02[0] + d13[1], d02[1] - d13[0])
        return out
    even, odd = complex_dft(values[0::2], sign), complex_dft(values[1::2], sign)
    turned = [rotate(odd[k], sign * k / n) for k in range(n // 2)]
    return [add(even[k], turned[k]) for k in range(n // 2)] + [
        sub(even[k], turned[k]) for k in range(n // 2)
    ]


def real_dft(values):
    n = len(values)
    if n == 1:
        return [values[0]]
    if n == 2:
        return [values[0] + values[1], values[0] - values[1]]
    even, odd = real_dft(values[0::2]), real_dft(values[1::2])
    out = [None] * (n // 2 + 1)
    out[0], out[n // 2] = even[0] + odd[0], even[0] - odd[0]
    for k in range(1, n // 4):
        turned = rotate(odd[k], -k / n)
        low, high = add(even[k], turned), sub(even[k], turned)
        out[k], out[n // 2 - k] = low, (high[0], -high[1])
    out[n // 4] = (even[n // 4], -odd[n // 4])
    return out


def real_inverse(entries):
    n = 2 * (len(entries) - 1)
    if n == 2:
        return [entries[0] + entries[1], entries[0] - entries[1]]
    even, odd = [None] * (n // 4 + 1), [None] * (n // 4 + 1)
    even[0], odd[0] = entries[0] + entries[n // 2], entries[0] - entries[n // 2]
    for k in range(1, n // 4):
        other = entries[n // 2 - k]
        other = (other[0], -other[1])
        even[k] = add(entries[k], other)
        odd[k] = rotate(sub(entries[k], other), k / n)
    middle = entries[n // 4]
    even[n // 4], odd[n // 4] = 2.0 * middle[0], -2.0 * middle[1]
    out = [None] * n
    out[0::2], out[1::2] = real_inverse(even), real_inverse(odd)
    return out


def circulant_tables():
    frequency = np.arange(SIDE)
    wavenumber = np.minimum(frequency, SIDE - frequency).astype(np.float64)
    screening = SIDE / 16.0
    values = screening / np.sqrt(
        wavenumber[:, None] ** 2 + wavenumber[None, :] ** 2 + screening * screening
    )
    values[0, 0] = 0.0
    cosines = np.cos(2 * np.pi * np.outer(frequency, frequency) / SIDE)
    taps = values[: SIDE // 2 + 1] @ cosines / (SIDE * SIDE)
    shift = (frequency[None, :] - frequency[:, None]) % SIDE
    tables = taps[:, shift].astype(np.float32)
    high = tables.astype(jnp.bfloat16)
    low = (tables - high.astype(np.float32)).astype(jnp.bfloat16)
    return jnp.asarray(np.concatenate([high, low], axis=2))


def fetches(step, slot, apart, arrays, cells_ref, in_sem):
    _, column, parts = step[2][apart]
    width = step[1] * SIDE
    return [
        pltpu.make_async_copy(
            arrays[which].at[:, pl.ds(column, width)],
            cells_ref.at[slot, apart, pl.ds(first, size), pl.ds(0, width)],
            in_sem.at[slot, apart],
        )
        for which, first, size in parts
    ]


def holder(step, apart):
    even_mask, odd_mask = step[2][apart][0]
    me, odd = lax.axis_index("grid"), lax.axis_index("pts") & 1
    if even_mask == odd_mask:
        return me ^ even_mask
    return me ^ (even_mask ^ (odd * (even_mask ^ odd_mask)))


def pick_from(step, apart, index_ref, cells):
    width, count = step[1] * SIDE, len(step[2])
    base = holder(step, apart) * (SIDE * SIDE // count) + step[0] * SIDE
    shape = (index_ref.shape[0], width)
    hot = lax.broadcasted_iota(jnp.int32, shape, 1) == index_ref[...] - base
    return lax.dot_general(
        jnp.where(hot, 1.0, 0.0).astype(jnp.bfloat16),
        cells,
        (((1,), (1,)), ((), ())),
        preferred_element_type=jnp.float32,
    )


def pick_kernel(steps, index_ref, *refs):
    *arrays, out_ref, cells_ref, total_ref, in_sem = refs
    count = len(steps[0][2])

    def start(at):
        for apart in range(count):
            for copy in fetches(steps[at], at % 2, apart, arrays, cells_ref, in_sem):
                copy.start()

    start(0)
    total_ref[...] = jnp.zeros_like(total_ref)
    for at, step in enumerate(steps):
        if at + 1 < len(steps):
            start(at + 1)
        for apart in range(count):
            for copy in fetches(step, at % 2, apart, arrays, cells_ref, in_sem):
                copy.wait()
            cells = cells_ref[at % 2, apart, :, : step[1] * SIDE]
            total_ref[...] += pick_from(step, apart, index_ref, cells)
    out_ref[...] = total_ref[...].astype(jnp.bfloat16)


def sheet_kernel(steps, pick_first, index_ref, picked_ref, far_tables_ref, *refs):
    *arrays, out_ref, chosen_ref, cells_ref, squared_ref, slots_ref, stage_ref = refs[:-4]
    tables_ref, in_sem, out_sem, table_sem = refs[-4:]
    table_copy = pltpu.make_async_copy(far_tables_ref, tables_ref, table_sem.at[0])
    count = len(steps[0][2])
    rows = SIDE // count
    points = picked_ref.shape[0]
    half = count // 2
    chunk = 8

    def start(at):
        for apart in range(count):
            for copy in fetches(steps[at], at % 2, apart, arrays, cells_ref, in_sem):
                copy.start()

    def wait(at, apart):
        for copy in fetches(steps[at], at % 2, apart, arrays, cells_ref, in_sem):
            copy.wait()

    for at in range(max(1, pick_first)):
        start(at)
    table_copy.start()
    if pick_first:
        total = picked_ref[...].astype(jnp.float32)
        for at in range(pick_first):
            for apart in range(count):
                wait(at, apart)
                cells = cells_ref[at, apart, :, : steps[at][1] * SIDE]
                total += pick_from(steps[at], apart, index_ref, cells)
        chosen_ref[...] = total.astype(jnp.bfloat16)
    else:
        chosen_ref[...] = picked_ref[...]

    for at, step in enumerate(steps):
        first_row, rows_here, _ = step
        width = rows_here * SIDE
        if max(1, pick_first) <= at + 1 < len(steps):
            start(at + 1)
        for apart in range(count):
            if at >= pick_first:
                wait(at, apart)
            pair = jnp.dot(
                chosen_ref[...],
                cells_ref[at % 2, apart, :, :width],
                preferred_element_type=jnp.float32,
            )
            squared_ref[holder(step, apart), :, :width] = pair * pair

        def spread(here, first_row=first_row, rows_here=rows_here):
            for within in range(rows_here):
                j = first_row + within
                lanes = pl.ds(within * SIDE, SIDE)
                entries = real_dft([squared_ref[g, here, lanes] for g in range(count)])
                slots_ref[0, j, here, :] = entries[0]
                slots_ref[count - 1, j, here, :] = entries[half]
                for k in range(1, half):
                    re, im = rotate(entries[k], -k * j / SIDE)
                    slots_ref[2 * k - 1, j, here, :] = re
                    slots_ref[2 * k, j, here, :] = im

        def one(at_chunk, carry):
            spread(pl.ds(pl.multiple_of(at_chunk * chunk, chunk), chunk))
            return carry

        lax.fori_loop(0, points // chunk, one, 0, unroll=min(2, points // chunk))

    table_copy.wait()

    def circulant(blocks, a):
        stacked = blocks[0] if len(blocks) == 1 else jnp.concatenate(blocks, axis=0)
        high = stacked.astype(jnp.bfloat16)
        low = (stacked - high.astype(jnp.float32)).astype(jnp.bfloat16)
        table = tables_ref[min(a, SIDE - a)]
        both = jnp.dot(
            jnp.concatenate([high, low], axis=1),
            jnp.concatenate([table, table], axis=0),
            preferred_element_type=jnp.float32,
        )
        return both[:, :SIDE] + both[:, SIDE:]

    def over_points(body, unroll):
        def one(at, carry):
            body(pl.ds(pl.multiple_of(at * chunk, chunk), chunk))
            return carry

        lax.fori_loop(0, points // chunk, one, 0, unroll=min(unroll, points // chunk))

    def apply(places, a):
        outs = circulant([slots_ref[s, j, :points, :] for s, j in places], a)
        for at, (s, j) in enumerate(places):
            slots_ref[s, j, :points, :] = outs[at * points : (at + 1) * points]

    def real_there(here):
        entries = real_dft([slots_ref[0, j, here, :] for j in range(rows)])
        slots_ref[0, 0, here, :] = entries[0]
        slots_ref[0, rows - 1, here, :] = entries[rows // 2]
        for k in range(1, rows // 2):
            slots_ref[0, 2 * k - 1, here, :], slots_ref[0, 2 * k, here, :] = entries[k]

    def real_back(here):
        entries = [slots_ref[0, 0, here, :]]
        for k in range(1, rows // 2):
            entries.append((slots_ref[0, 2 * k - 1, here, :], slots_ref[0, 2 * k, here, :]))
        entries.append(slots_ref[0, rows - 1, here, :])
        for j, value in enumerate(real_inverse(entries)):
            slots_ref[0, j, here, :] = value

    over_points(real_there, 4)
    apply([(0, 0)], 0)
    apply([(0, rows - 1)], SIDE // 2)
    for k in range(1, rows // 2):
        apply([(0, 2 * k - 1), (0, 2 * k)], count * k)
    over_points(real_back, 4)

    last = count - 1
    short = rows // 2

    def odd_there(here):
        values = [
            rotate((slots_ref[last, j, here, :], -slots_ref[last, j + short, here, :]), -j / (2 * rows))
            for j in range(short)
        ]
        for k, (re, im) in enumerate(complex_dft(values, -1)):
            slots_ref[last, 2 * k, here, :] = re
            slots_ref[last, 2 * k + 1, here, :] = im

    def odd_back(here):
        values = [
            (slots_ref[last, 2 * k, here, :], slots_ref[last, 2 * k + 1, here, :])
            for k in range(short)
        ]
        for j, value in enumerate(complex_dft(values, 1)):
            re, im = rotate(value, j / (2 * rows))
            slots_ref[last, j, here, :] = 2.0 * re
            slots_ref[last, j + short, here, :] = -2.0 * im

    over_points(odd_there, 4)
    for k in range(short):
        apply([(last, 2 * k), (last, 2 * k + 1)], half + 2 * count * k)
    over_points(odd_back, 4)

    for k in range(1, half):
        re_slot, im_slot = 2 * k - 1, 2 * k

        def complex_there(here, sign=-1):
            values = [
                (slots_ref[re_slot, j, here, :], slots_ref[im_slot, j, here, :])
                for j in range(rows)
            ]
            for j, (re, im) in enumerate(complex_dft(values, sign)):
                slots_ref[re_slot, j, here, :] = re
                slots_ref[im_slot, j, here, :] = im

        over_points(complex_there, 4)
        for a2 in range(rows):
            apply([(re_slot, a2), (im_slot, a2)], k + count * a2)
        over_points(functools.partial(complex_there, sign=1), 4)

    def put(j, slot):
        return [
            pltpu.make_async_copy(
                stage_ref.at[slot, g], out_ref.at[:, rows * g + j, :], out_sem.at[slot]
            )
            for g in range(count)
        ]

    for j in range(rows):
        slot = j % STAGES
        if j >= STAGES:
            for copy in put(j - STAGES, slot):
                copy.wait()

        def gather_back(here):
            entries = [slots_ref[0, j, here, :]]
            for k in range(1, half):
                entries.append(
                    rotate(
                        (slots_ref[2 * k - 1, j, here, :], slots_ref[2 * k, j, here, :]),
                        k * j / SIDE,
                    )
                )
            entries.append(slots_ref[count - 1, j, here, :])
            for g, value in enumerate(real_inverse(entries)):
                stage_ref[slot, g, here, :] = value

        over_points(gather_back, 4)
        for copy in put(j, slot):
            copy.start()
    for j in range(max(rows - STAGES, 0), rows):
        for copy in put(j, j % STAGES):
            copy.wait()


VMEM_SPEC = pl.BlockSpec(memory_space=pltpu.VMEM)
ANY_SPEC = pl.BlockSpec(memory_space=pl.ANY)


def flatten(steps):
    arrays, plan = [], []
    for first_row, rows_here, entries in steps:
        numbered = []
        for masks, column, parts in entries:
            for array, _ in parts:
                if not any(array is known for known in arrays):
                    arrays.append(array)
            which = [next(i for i, known in enumerate(arrays) if known is array) for array, _ in parts]
            numbered.append(
                (masks, column, tuple((w, first, a.shape[0]) for w, (a, first) in zip(which, parts)))
            )
        plan.append((first_row, rows_here, tuple(numbered)))
    return tuple(plan), arrays


def cell_buffers(plan, orbital_count):
    widest = max(rows_here for _, rows_here, _ in plan) * SIDE
    return pltpu.VMEM((min(2, len(plan)), len(plan[0][2]), orbital_count, widest), jnp.bfloat16)


def pick_cells(index, orbital_count, steps, us=0):
    plan, arrays = flatten(steps)
    count = len(plan[0][2])
    shape = (index.shape[0], orbital_count)
    return pl.pallas_call(
        functools.partial(pick_kernel, plan),
        in_specs=[VMEM_SPEC] + [ANY_SPEC] * len(arrays),
        out_specs=VMEM_SPEC,
        out_shape=jax.ShapeDtypeStruct(shape, jnp.bfloat16),
        scratch_shapes=[
            cell_buffers(plan, orbital_count),
            pltpu.VMEM(shape, jnp.float32),
            pltpu.SemaphoreType.DMA((2, count)),
        ],
        compiler_params=pltpu.CompilerParams(vmem_limit_bytes=VMEM_BYTES),
        cost_estimate=pl.CostEstimate(flops=us * 5 * 10**8, bytes_accessed=0, transcendentals=0),
    )(index, *arrays)


def screen_sheets(index, picked, tables, steps, pick_first):
    points, orbital_count = picked.shape
    plan, arrays = flatten(steps)
    count = len(plan[0][2])
    rows = SIDE // count
    widest = max(rows_here for _, rows_here, _ in plan) * SIDE
    return pl.pallas_call(
        functools.partial(sheet_kernel, plan, pick_first),
        in_specs=[VMEM_SPEC] * 2 + [ANY_SPEC] * (1 + len(arrays)),
        out_specs=ANY_SPEC,
        out_shape=jax.ShapeDtypeStruct((points, SIDE, SIDE), jnp.float32),
        scratch_shapes=[
            pltpu.VMEM((points, orbital_count), jnp.bfloat16),
            cell_buffers(plan, orbital_count),
            pltpu.VMEM((count, points, widest), jnp.float32),
            pltpu.VMEM((count, rows, points + 8, SIDE), jnp.float32),
            pltpu.VMEM((STAGES, count, points, SIDE), jnp.float32),
            pltpu.VMEM(tables.shape, tables.dtype),
            pltpu.SemaphoreType.DMA((2, count)),
            pltpu.SemaphoreType.DMA((STAGES,)),
            pltpu.SemaphoreType.DMA((1,)),
        ],
        compiler_params=pltpu.CompilerParams(vmem_limit_bytes=VMEM_BYTES),
    )(index, picked, tables, *arrays)


def swap(array, mask):
    count = lax.axis_size("grid")
    return lax.ppermute(array, "grid", [(i, i ^ mask) for i in range(count)])


def routes(bits):
    cut = (bits - 1) // 2
    links = list(range(1, bits))
    return links, links[cut:] + links[:cut]


class Order:
    def __init__(self, seed):
        self.token = seed

    def start(self, move, array, *arguments):
        array, _ = lax.optimization_barrier((array, self.token))
        return move(array, *arguments)

    def wait(self, *arrays):
        self.token, *_ = lax.optimization_barrier((self.token, *arrays))


def gather_cells(orbitals):
    count = lax.axis_size("grid")
    bits = count.bit_length() - 1
    middle = orbitals.shape[0] // 2
    held = {0: [(orbitals, 0)]}
    pieces = ({0: orbitals[:middle]}, {0: orbitals[middle:]})
    for route, have in zip(routes(bits), pieces):
        for bit in route:
            for known in sorted(have):
                have[known | 1 << bit] = swap(have[known], 1 << bit)
    for known in pieces[0]:
        if known:
            held[known] = [(pieces[0][known], 0), (pieces[1][known], middle)]
    for known in sorted(held):
        held[known | 1] = [(swap(array, 1), first) for array, first in held[known]]
    rows = SIDE // count
    return [
        (j, 1, [((d, d), j * SIDE, held[d]) for d in range(count)]) for j in range(rows)
    ]


CORE, NEAR, FAR = 1, 2, 4
SCRIPT = ("F0", "F1", "B", "P0", "F2", "P1", "F3", "S0", "P2", "S1", "W", "X3", "V2", "P3", "S2", "K012:0", "S3")
PIECE_ROWS = (4, 4, 4, 4)


def exchange(array, masks, across):
    count, planes = lax.axis_size("grid"), lax.axis_size("pts")
    pairs = [
        (g * planes + z, (g ^ masks[z & 1]) * planes + (z ^ across))
        for g in range(count)
        for z in range(planes)
    ]
    return lax.ppermute(array, ("grid", "pts"), pairs)


def four_chips(orbitals, index, seed, tables):
    order = Order(seed)
    ends = [sum(PIECE_ROWS[:p]) for p in range(len(PIECE_ROWS) + 1)]
    first, far, core = {}, {}, {}

    def send_first(p):
        source = lax.optimization_barrier((orbitals, order.token))[0]
        piece = source[:, ends[p] * SIDE : ends[p + 1] * SIDE]
        first[p] = exchange(piece, (NEAR, FAR), 0)

    def pass_on(p):
        order.wait(first[p])
        far[p] = (
            order.start(exchange, first[p], (FAR, NEAR), 0),
            order.start(exchange, first[p], (0, 0), 1),
        )
        core[p] = [order.start(swap, first[p], CORE)]

    def share(p):
        order.wait(*far[p])
        core[p] += [order.start(swap, array, CORE) for array in far[p]]

    def step(p):
        order.wait(*core[p])
        entry = [
            ((0, 0), ends[p] * SIDE, [(orbitals, 0)]),
            ((CORE, CORE), ends[p] * SIDE, [(sibling, 0)]),
        ]
        arrays = (first[p], *far[p])
        for masks, array, other in zip(((NEAR, FAR), (NEAR | FAR,) * 2, (FAR, NEAR)), arrays, core[p]):
            entry.append((masks, 0, [(array, 0)]))
            entry.append((tuple(m | CORE for m in masks), 0, [(other, 0)]))
        return (ends[p], PIECE_ROWS[p], entry)

    steps, picks = {}, []
    for word in SCRIPT:
        op, arg = word[0], word[1:]
        if op == "F":
            send_first(int(arg))
        elif op == "P":
            pass_on(int(arg))
        elif op == "S":
            share(int(arg))
        elif op == "V":
            order.wait(*far[int(arg)])
        elif op == "X":
            order.wait(first[int(arg)])
        elif op == "B":
            sibling = order.start(swap, orbitals, CORE)
        elif op == "W":
            order.wait(sibling)
        elif op == "K":
            ids, cost = arg.split(":")
            for p in ids:
                steps[int(p)] = step(int(p))
            picks.append(pick_cells(index, orbitals.shape[0], [steps[int(p)] for p in ids], int(cost)))
            order.wait(picks[-1])
    left = [step(p) for p in range(len(PIECE_ROWS)) if p not in steps]
    picked = functools.reduce(lambda x, y: x + y, picks)
    return screen_sheets(index, picked, tables, left + [steps[p] for p in sorted(steps)], len(left))


def shards(orbitals, point_index):
    count = lax.axis_size("grid")
    points = point_index.shape[0] // count
    index = lax.dynamic_slice_in_dim(point_index, lax.axis_index("grid") * points, points)[:, None]
    tables = circulant_tables()
    if count == 8 and lax.axis_size("pts") % 2 == 0:
        return four_chips(orbitals, index, point_index[:1], tables)[None]
    steps = gather_cells(orbitals)
    picked = pick_cells(index, orbitals.shape[0], steps)
    return screen_sheets(index, picked, tables, steps, 0)[None]


def solution(mesh):
    in_specs = (P(None, "grid"), P("pts"))
    out_specs = P("pts", "grid", None, None)
    return jax.shard_map(shards, mesh=mesh, in_specs=in_specs, out_specs=out_specs, check_vma=False)
```

```python
import functools
import math

import jax
import jax.numpy as jnp
import numpy as np
from jax import lax
from jax.experimental import pallas as pl
from jax.experimental.pallas import tpu as pltpu
from jax.sharding import PartitionSpec as P

SIDE = 128
VMEM_BYTES = 63 * 2**20
STAGES = 4


def rotate(value, turn):
    re, im = value
    turn = turn % 1.0
    if turn == 0.0:
        return (re, im)
    if turn == 0.25:
        return (-im, re)
    if turn == 0.5:
        return (-re, -im)
    if turn == 0.75:
        return (im, -re)
    cos, sin = math.cos(2 * math.pi * turn), math.sin(2 * math.pi * turn)
    if turn in (0.125, 0.375, 0.625, 0.875):
        plus, minus = (re + im) * abs(cos), (re - im) * abs(cos)
        if turn == 0.125:
            return (minus, plus)
        if turn == 0.375:
            return (-plus, minus)
        if turn == 0.625:
            return (-minus, -plus)
        return (plus, -minus)
    return (re * cos - im * sin, re * sin + im * cos)


def add(a, b):
    return (a[0] + b[0], a[1] + b[1])


def sub(a, b):
    return (a[0] - b[0], a[1] - b[1])


def complex_dft(values, sign):
    n = len(values)
    if n == 1:
        return list(values)
    if n == 2:
        return [add(values[0], values[1]), sub(values[0], values[1])]
    if n % 4 == 0:
        parts = [complex_dft(values[r::4], sign) for r in range(4)]
        out = [None] * n
        quarter = n // 4
        for k in range(quarter):
            t0, t1, t2, t3 = (rotate(parts[r][k], sign * r * k / n) for r in range(4))
            s02, d02 = add(t0, t2), sub(t0, t2)
            s13, d13 = add(t1, t3), sub(t1, t3)
            out[k] = add(s02, s13)
            out[k + 2 * quarter] = sub(s02, s13)
            if sign < 0:
                out[k + quarter] = (d02[0] + d13[1], d02[1] - d13[0])
                out[k + 3 * quarter] = (d02[0] - d13[1], d02[1] + d13[0])
            else:
                out[k + quarter] = (d02[0] - d13[1], d02[1] + d13[0])
                out[k + 3 * quarter] = (d02[0] + d13[1], d02[1] - d13[0])
        return out
    even, odd = complex_dft(values[0::2], sign), complex_dft(values[1::2], sign)
    turned = [rotate(odd[k], sign * k / n) for k in range(n // 2)]
    return [add(even[k], turned[k]) for k in range(n // 2)] + [
        sub(even[k], turned[k]) for k in range(n // 2)
    ]


def real_dft(values):
    n = len(values)
    if n == 1:
        return [values[0]]
    if n == 2:
        return [values[0] + values[1], values[0] - values[1]]
    even, odd = real_dft(values[0::2]), real_dft(values[1::2])
    out = [None] * (n // 2 + 1)
    out[0], out[n // 2] = even[0] + odd[0], even[0] - odd[0]
    for k in range(1, n // 4):
        turned = rotate(odd[k], -k / n)
        low, high = add(even[k], turned), sub(even[k], turned)
        out[k], out[n // 2 - k] = low, (high[0], -high[1])
    out[n // 4] = (even[n // 4], -odd[n // 4])
    return out


def real_inverse(entries):
    n = 2 * (len(entries) - 1)
    if n == 2:
        return [entries[0] + entries[1], entries[0] - entries[1]]
    even, odd = [None] * (n // 4 + 1), [None] * (n // 4 + 1)
    even[0], odd[0] = entries[0] + entries[n // 2], entries[0] - entries[n // 2]
    for k in range(1, n // 4):
        other = entries[n // 2 - k]
        other = (other[0], -other[1])
        even[k] = add(entries[k], other)
        odd[k] = rotate(sub(entries[k], other), k / n)
    middle = entries[n // 4]
    even[n // 4], odd[n // 4] = 2.0 * middle[0], -2.0 * middle[1]
    out = [None] * n
    out[0::2], out[1::2] = real_inverse(even), real_inverse(odd)
    return out


def circulant_tables():
    frequency = np.arange(SIDE)
    wavenumber = np.minimum(frequency, SIDE - frequency).astype(np.float64)
    screening = SIDE / 16.0
    values = screening / np.sqrt(
        wavenumber[:, None] ** 2 + wavenumber[None, :] ** 2 + screening * screening
    )
    values[0, 0] = 0.0
    cosines = np.cos(2 * np.pi * np.outer(frequency, frequency) / SIDE)
    taps = values[: SIDE // 2 + 1] @ cosines / (SIDE * SIDE)
    shift = (frequency[None, :] - frequency[:, None]) % SIDE
    tables = taps[:, shift].astype(np.float32)
    high = tables.astype(jnp.bfloat16)
    low = (tables - high.astype(np.float32)).astype(jnp.bfloat16)
    return jnp.asarray(np.concatenate([high, low], axis=2))


def fetches(step, slot, apart, arrays, cells_ref, in_sem):
    _, column, parts = step[2][apart]
    width = step[1] * SIDE
    return [
        pltpu.make_async_copy(
            arrays[which].at[:, pl.ds(column, width)],
            cells_ref.at[slot, apart, pl.ds(first, size), pl.ds(0, width)],
            in_sem.at[slot, apart],
        )
        for which, first, size in parts
    ]


def holder(step, apart):
    even_mask, odd_mask = step[2][apart][0]
    me, odd = lax.axis_index("grid"), lax.axis_index("pts") & 1
    if even_mask == odd_mask:
        return me ^ even_mask
    return me ^ (even_mask ^ (odd * (even_mask ^ odd_mask)))


def pick_from(step, apart, index_ref, cells):
    width, count = step[1] * SIDE, len(step[2])
    base = holder(step, apart) * (SIDE * SIDE // count) + step[0] * SIDE
    shape = (index_ref.shape[0], width)
    hot = lax.broadcasted_iota(jnp.int32, shape, 1) == index_ref[...] - base
    return lax.dot_general(
        jnp.where(hot, 1.0, 0.0).astype(jnp.bfloat16),
        cells,
        (((1,), (1,)), ((), ())),
        preferred_element_type=jnp.float32,
    )


def pick_kernel(steps, index_ref, *refs):
    *arrays, out_ref, cells_ref, total_ref, in_sem = refs
    count = len(steps[0][2])

    def start(at):
        for apart in range(count):
            for copy in fetches(steps[at], at % 2, apart, arrays, cells_ref, in_sem):
                copy.start()

    start(0)
    total_ref[...] = jnp.zeros_like(total_ref)
    for at, step in enumerate(steps):
        if at + 1 < len(steps):
            start(at + 1)
        for apart in range(count):
            for copy in fetches(step, at % 2, apart, arrays, cells_ref, in_sem):
                copy.wait()
            cells = cells_ref[at % 2, apart, :, : step[1] * SIDE]
            total_ref[...] += pick_from(step, apart, index_ref, cells)
    out_ref[...] = total_ref[...].astype(jnp.bfloat16)


def sheet_kernel(steps, pick_first, index_ref, picked_ref, far_tables_ref, *refs):
    *arrays, out_ref, chosen_ref, cells_ref, squared_ref, slots_ref, stage_ref = refs[:-4]
    tables_ref, in_sem, out_sem, table_sem = refs[-4:]
    table_copy = pltpu.make_async_copy(far_tables_ref, tables_ref, table_sem.at[0])
    count = len(steps[0][2])
    rows = SIDE // count
    points = picked_ref.shape[0]
    half = count // 2
    chunk = 8

    def start(at):
        for apart in range(count):
            for copy in fetches(steps[at], at % 2, apart, arrays, cells_ref, in_sem):
                copy.start()

    def wait(at, apart):
        for copy in fetches(steps[at], at % 2, apart, arrays, cells_ref, in_sem):
            copy.wait()

    for at in range(max(1, pick_first)):
        start(at)
    table_copy.start()
    if pick_first:
        total = picked_ref[...].astype(jnp.float32)
        for at in range(pick_first):
            for apart in range(count):
                wait(at, apart)
                cells = cells_ref[at, apart, :, : steps[at][1] * SIDE]
                total += pick_from(steps[at], apart, index_ref, cells)
        chosen_ref[...] = total.astype(jnp.bfloat16)
    else:
        chosen_ref[...] = picked_ref[...]

    for at, step in enumerate(steps):
        first_row, rows_here, _ = step
        width = rows_here * SIDE
        if max(1, pick_first) <= at + 1 < len(steps):
            start(at + 1)
        for apart in range(count):
            if at >= pick_first:
                wait(at, apart)
            pair = jnp.dot(
                chosen_ref[...],
                cells_ref[at % 2, apart, :, :width],
                preferred_element_type=jnp.float32,
            )
            squared_ref[holder(step, apart), :, :width] = pair * pair

        def spread(here, first_row=first_row, rows_here=rows_here):
            for within in range(rows_here):
                j = first_row + within
                lanes = pl.ds(within * SIDE, SIDE)
                entries = real_dft([squared_ref[g, here, lanes] for g in range(count)])
                slots_ref[0, j, here, :] = entries[0]
                slots_ref[count - 1, j, here, :] = entries[half]
                for k in range(1, half):
                    re, im = rotate(entries[k], -k * j / SIDE)
                    slots_ref[2 * k - 1, j, here, :] = re
                    slots_ref[2 * k, j, here, :] = im

        def one(at_chunk, carry):
            spread(pl.ds(pl.multiple_of(at_chunk * chunk, chunk), chunk))
            return carry

        lax.fori_loop(0, points // chunk, one, 0, unroll=min(2, points // chunk))

    table_copy.wait()

    def circulant(blocks, a):
        stacked = blocks[0] if len(blocks) == 1 else jnp.concatenate(blocks, axis=0)
        high = stacked.astype(jnp.bfloat16)
        low = (stacked - high.astype(jnp.float32)).astype(jnp.bfloat16)
        table = tables_ref[min(a, SIDE - a)]
        both = jnp.dot(
            jnp.concatenate([high, low], axis=1),
            jnp.concatenate([table, table], axis=0),
            preferred_element_type=jnp.float32,
        )
        return both[:, :SIDE] + both[:, SIDE:]

    def over_points(body, unroll):
        def one(at, carry):
            body(pl.ds(pl.multiple_of(at * chunk, chunk), chunk))
            return carry

        lax.fori_loop(0, points // chunk, one, 0, unroll=min(unroll, points // chunk))

    def apply(places, a):
        outs = circulant([slots_ref[s, j, :points, :] for s, j in places], a)
        for at, (s, j) in enumerate(places):
            slots_ref[s, j, :points, :] = outs[at * points : (at + 1) * points]

    def real_there(here):
        entries = real_dft([slots_ref[0, j, here, :] for j in range(rows)])
        slots_ref[0, 0, here, :] = entries[0]
        slots_ref[0, rows - 1, here, :] = entries[rows // 2]
        for k in range(1, rows // 2):
            slots_ref[0, 2 * k - 1, here, :], slots_ref[0, 2 * k, here, :] = entries[k]

    def real_back(here):
        entries = [slots_ref[0, 0, here, :]]
        for k in range(1, rows // 2):
            entries.append((slots_ref[0, 2 * k - 1, here, :], slots_ref[0, 2 * k, here, :]))
        entries.append(slots_ref[0, rows - 1, here, :])
        for j, value in enumerate(real_inverse(entries)):
            slots_ref[0, j, here, :] = value

    over_points(real_there, 4)
    apply([(0, 0)], 0)
    apply([(0, rows - 1)], SIDE // 2)
    for k in range(1, rows // 2):
        apply([(0, 2 * k - 1), (0, 2 * k)], count * k)
    over_points(real_back, 4)

    last = count - 1
    short = rows // 2

    def odd_there(here):
        values = [
            rotate((slots_ref[last, j, here, :], -slots_ref[last, j + short, here, :]), -j / (2 * rows))
            for j in range(short)
        ]
        for k, (re, im) in enumerate(complex_dft(values, -1)):
            slots_ref[last, 2 * k, here, :] = re
            slots_ref[last, 2 * k + 1, here, :] = im

    def odd_back(here):
        values = [
            (slots_ref[last, 2 * k, here, :], slots_ref[last, 2 * k + 1, here, :])
            for k in range(short)
        ]
        for j, value in enumerate(complex_dft(values, 1)):
            re, im = rotate(value, j / (2 * rows))
            slots_ref[last, j, here, :] = 2.0 * re
            slots_ref[last, j + short, here, :] = -2.0 * im

    over_points(odd_there, 4)
    for k in range(short):
        apply([(last, 2 * k), (last, 2 * k + 1)], half + 2 * count * k)
    over_points(odd_back, 4)

    for k in range(1, half):
        re_slot, im_slot = 2 * k - 1, 2 * k

        def complex_there(here, sign=-1):
            values = [
                (slots_ref[re_slot, j, here, :], slots_ref[im_slot, j, here, :])
                for j in range(rows)
            ]
            for j, (re, im) in enumerate(complex_dft(values, sign)):
                slots_ref[re_slot, j, here, :] = re
                slots_ref[im_slot, j, here, :] = im

        over_points(complex_there, 4)
        for a2 in range(rows):
            apply([(re_slot, a2), (im_slot, a2)], k + count * a2)
        over_points(functools.partial(complex_there, sign=1), 4)

    def put(j, slot):
        return [
            pltpu.make_async_copy(
                stage_ref.at[slot, g], out_ref.at[:, rows * g + j, :], out_sem.at[slot]
            )
            for g in range(count)
        ]

    for j in range(rows):
        slot = j % STAGES
        if j >= STAGES:
            for copy in put(j - STAGES, slot):
                copy.wait()

        def gather_back(here):
            entries = [slots_ref[0, j, here, :]]
            for k in range(1, half):
                entries.append(
                    rotate(
                        (slots_ref[2 * k - 1, j, here, :], slots_ref[2 * k, j, here, :]),
                        k * j / SIDE,
                    )
                )
            entries.append(slots_ref[count - 1, j, here, :])
            for g, value in enumerate(real_inverse(entries)):
                stage_ref[slot, g, here, :] = value

        over_points(gather_back, 4)
        for copy in put(j, slot):
            copy.start()
    for j in range(max(rows - STAGES, 0), rows):
        for copy in put(j, j % STAGES):
            copy.wait()


VMEM_SPEC = pl.BlockSpec(memory_space=pltpu.VMEM)
ANY_SPEC = pl.BlockSpec(memory_space=pl.ANY)


def flatten(steps):
    arrays, plan = [], []
    for first_row, rows_here, entries in steps:
        numbered = []
        for masks, column, parts in entries:
            for array, _ in parts:
                if not any(array is known for known in arrays):
                    arrays.append(array)
            which = [next(i for i, known in enumerate(arrays) if known is array) for array, _ in parts]
            numbered.append(
                (masks, column, tuple((w, first, a.shape[0]) for w, (a, first) in zip(which, parts)))
            )
        plan.append((first_row, rows_here, tuple(numbered)))
    return tuple(plan), arrays


def cell_buffers(plan, orbital_count):
    widest = max(rows_here for _, rows_here, _ in plan) * SIDE
    return pltpu.VMEM((min(2, len(plan)), len(plan[0][2]), orbital_count, widest), jnp.bfloat16)


def pick_cells(index, orbital_count, steps, us=0):
    plan, arrays = flatten(steps)
    count = len(plan[0][2])
    shape = (index.shape[0], orbital_count)
    return pl.pallas_call(
        functools.partial(pick_kernel, plan),
        in_specs=[VMEM_SPEC] + [ANY_SPEC] * len(arrays),
        out_specs=VMEM_SPEC,
        out_shape=jax.ShapeDtypeStruct(shape, jnp.bfloat16),
        scratch_shapes=[
            cell_buffers(plan, orbital_count),
            pltpu.VMEM(shape, jnp.float32),
            pltpu.SemaphoreType.DMA((2, count)),
        ],
        compiler_params=pltpu.CompilerParams(vmem_limit_bytes=VMEM_BYTES),
        cost_estimate=pl.CostEstimate(flops=us * 5 * 10**8, bytes_accessed=0, transcendentals=0),
    )(index, *arrays)


def screen_sheets(index, picked, tables, steps, pick_first):
    points, orbital_count = picked.shape
    plan, arrays = flatten(steps)
    count = len(plan[0][2])
    rows = SIDE // count
    widest = max(rows_here for _, rows_here, _ in plan) * SIDE
    return pl.pallas_call(
        functools.partial(sheet_kernel, plan, pick_first),
        in_specs=[VMEM_SPEC] * 2 + [ANY_SPEC] * (1 + len(arrays)),
        out_specs=ANY_SPEC,
        out_shape=jax.ShapeDtypeStruct((points, SIDE, SIDE), jnp.float32),
        scratch_shapes=[
            pltpu.VMEM((points, orbital_count), jnp.bfloat16),
            cell_buffers(plan, orbital_count),
            pltpu.VMEM((count, points, widest), jnp.float32),
            pltpu.VMEM((count, rows, points + 8, SIDE), jnp.float32),
            pltpu.VMEM((STAGES, count, points, SIDE), jnp.float32),
            pltpu.VMEM(tables.shape, tables.dtype),
            pltpu.SemaphoreType.DMA((2, count)),
            pltpu.SemaphoreType.DMA((STAGES,)),
            pltpu.SemaphoreType.DMA((1,)),
        ],
        compiler_params=pltpu.CompilerParams(vmem_limit_bytes=VMEM_BYTES),
    )(index, picked, tables, *arrays)


def swap(array, mask):
    count = lax.axis_size("grid")
    return lax.ppermute(array, "grid", [(i, i ^ mask) for i in range(count)])


def routes(bits):
    cut = (bits - 1) // 2
    links = list(range(1, bits))
    return links, links[cut:] + links[:cut]


class Order:
    def __init__(self, seed):
        self.token = seed

    def start(self, move, array, *arguments):
        array, _ = lax.optimization_barrier((array, self.token))
        return move(array, *arguments)

    def wait(self, *arrays):
        self.token, *_ = lax.optimization_barrier((self.token, *arrays))


def gather_cells(orbitals):
    count = lax.axis_size("grid")
    bits = count.bit_length() - 1
    middle = orbitals.shape[0] // 2
    held = {0: [(orbitals, 0)]}
    pieces = ({0: orbitals[:middle]}, {0: orbitals[middle:]})
    for route, have in zip(routes(bits), pieces):
        for bit in route:
            for known in sorted(have):
                have[known | 1 << bit] = swap(have[known], 1 << bit)
    for known in pieces[0]:
        if known:
            held[known] = [(pieces[0][known], 0), (pieces[1][known], middle)]
    for known in sorted(held):
        held[known | 1] = [(swap(array, 1), first) for array, first in held[known]]
    rows = SIDE // count
    return [
        (j, 1, [((d, d), j * SIDE, held[d]) for d in range(count)]) for j in range(rows)
    ]


CORE, NEAR, FAR = 1, 2, 4
SCRIPT = ("F0", "F1", "B", "P0", "F2", "P1", "F3", "S0", "P2", "W", "S1", "X3", "V2", "P3", "S2", "K012:0", "S3")
PIECE_ROWS = (4, 4, 4, 4)


def exchange(array, masks, across):
    count, planes = lax.axis_size("grid"), lax.axis_size("pts")
    pairs = [
        (g * planes + z, (g ^ masks[z & 1]) * planes + (z ^ across))
        for g in range(count)
        for z in range(planes)
    ]
    return lax.ppermute(array, ("grid", "pts"), pairs)


def four_chips(orbitals, index, seed, tables):
    order = Order(seed)
    ends = [sum(PIECE_ROWS[:p]) for p in range(len(PIECE_ROWS) + 1)]
    first, far, core = {}, {}, {}

    def send_first(p):
        source = lax.optimization_barrier((orbitals, order.token))[0]
        piece = source[:, ends[p] * SIDE : ends[p + 1] * SIDE]
        first[p] = exchange(piece, (NEAR, FAR), 0)

    def pass_on(p):
        order.wait(first[p])
        far[p] = (
            order.start(exchange, first[p], (FAR, NEAR), 0),
            order.start(exchange, first[p], (0, 0), 1),
        )
        core[p] = [order.start(swap, first[p], CORE)]

    def share(p):
        order.wait(*far[p])
        core[p] += [order.start(swap, array, CORE) for array in far[p]]

    def step(p):
        order.wait(*core[p])
        entry = [
            ((0, 0), ends[p] * SIDE, [(orbitals, 0)]),
            ((CORE, CORE), ends[p] * SIDE, [(sibling, 0)]),
        ]
        arrays = (first[p], *far[p])
        for masks, array, other in zip(((NEAR, FAR), (NEAR | FAR,) * 2, (FAR, NEAR)), arrays, core[p]):
            entry.append((masks, 0, [(array, 0)]))
            entry.append((tuple(m | CORE for m in masks), 0, [(other, 0)]))
        return (ends[p], PIECE_ROWS[p], entry)

    steps, picks = {}, []
    for word in SCRIPT:
        op, arg = word[0], word[1:]
        if op == "F":
            send_first(int(arg))
        elif op == "P":
            pass_on(int(arg))
        elif op == "S":
            share(int(arg))
        elif op == "V":
            order.wait(*far[int(arg)])
        elif op == "X":
            order.wait(first[int(arg)])
        elif op == "B":
            sibling = order.start(swap, orbitals, CORE)
        elif op == "W":
            order.wait(sibling)
        elif op == "K":
            ids, cost = arg.split(":")
            for p in ids:
                steps[int(p)] = step(int(p))
            picks.append(pick_cells(index, orbitals.shape[0], [steps[int(p)] for p in ids], int(cost)))
            order.wait(picks[-1])
    left = [step(p) for p in range(len(PIECE_ROWS)) if p not in steps]
    picked = functools.reduce(lambda x, y: x + y, picks)
    return screen_sheets(index, picked, tables, left + [steps[p] for p in sorted(steps)], len(left))


def shards(orbitals, point_index):
    count = lax.axis_size("grid")
    points = point_index.shape[0] // count
    index = lax.dynamic_slice_in_dim(point_index, lax.axis_index("grid") * points, points)[:, None]
    tables = circulant_tables()
    if count == 8 and lax.axis_size("pts") % 2 == 0:
        return four_chips(orbitals, index, point_index[:1], tables)[None]
    steps = gather_cells(orbitals)
    picked = pick_cells(index, orbitals.shape[0], steps)
    return screen_sheets(index, picked, tables, steps, 0)[None]


def solution(mesh):
    in_specs = (P(None, "grid"), P("pts"))
    out_specs = P("pts", "grid", None, None)
    return jax.shard_map(shards, mesh=mesh, in_specs=in_specs, out_specs=out_specs, check_vma=False)
```

```python
import functools
import math

import jax
import jax.numpy as jnp
import numpy as np
from jax import lax
from jax.experimental import pallas as pl
from jax.experimental.pallas import tpu as pltpu
from jax.sharding import PartitionSpec as P

SIDE = 128
VMEM_BYTES = 63 * 2**20
STAGES = 4


def rotate(value, turn):
    re, im = value
    turn = turn % 1.0
    if turn == 0.0:
        return (re, im)
    if turn == 0.25:
        return (-im, re)
    if turn == 0.5:
        return (-re, -im)
    if turn == 0.75:
        return (im, -re)
    cos, sin = math.cos(2 * math.pi * turn), math.sin(2 * math.pi * turn)
    if turn in (0.125, 0.375, 0.625, 0.875):
        plus, minus = (re + im) * abs(cos), (re - im) * abs(cos)
        if turn == 0.125:
            return (minus, plus)
        if turn == 0.375:
            return (-plus, minus)
        if turn == 0.625:
            return (-minus, -plus)
        return (plus, -minus)
    return (re * cos - im * sin, re * sin + im * cos)


def add(a, b):
    return (a[0] + b[0], a[1] + b[1])


def sub(a, b):
    return (a[0] - b[0], a[1] - b[1])


def complex_dft(values, sign):
    n = len(values)
    if n == 1:
        return list(values)
    if n == 2:
        return [add(values[0], values[1]), sub(values[0], values[1])]
    if n % 4 == 0:
        parts = [complex_dft(values[r::4], sign) for r in range(4)]
        out = [None] * n
        quarter = n // 4
        for k in range(quarter):
            t0, t1, t2, t3 = (rotate(parts[r][k], sign * r * k / n) for r in range(4))
            s02, d02 = add(t0, t2), sub(t0, t2)
            s13, d13 = add(t1, t3), sub(t1, t3)
            out[k] = add(s02, s13)
            out[k + 2 * quarter] = sub(s02, s13)
            if sign < 0:
                out[k + quarter] = (d02[0] + d13[1], d02[1] - d13[0])
                out[k + 3 * quarter] = (d02[0] - d13[1], d02[1] + d13[0])
            else:
                out[k + quarter] = (d02[0] - d13[1], d02[1] + d13[0])
                out[k + 3 * quarter] = (d02[0] + d13[1], d02[1] - d13[0])
        return out
    even, odd = complex_dft(values[0::2], sign), complex_dft(values[1::2], sign)
    turned = [rotate(odd[k], sign * k / n) for k in range(n // 2)]
    return [add(even[k], turned[k]) for k in range(n // 2)] + [
        sub(even[k], turned[k]) for k in range(n // 2)
    ]


def real_dft(values):
    n = len(values)
    if n == 1:
        return [values[0]]
    if n == 2:
        return [values[0] + values[1], values[0] - values[1]]
    even, odd = real_dft(values[0::2]), real_dft(values[1::2])
    out = [None] * (n // 2 + 1)
    out[0], out[n // 2] = even[0] + odd[0], even[0] - odd[0]
    for k in range(1, n // 4):
        turned = rotate(odd[k], -k / n)
        low, high = add(even[k], turned), sub(even[k], turned)
        out[k], out[n // 2 - k] = low, (high[0], -high[1])
    out[n // 4] = (even[n // 4], -odd[n // 4])
    return out


def real_inverse(entries):
    n = 2 * (len(entries) - 1)
    if n == 2:
        return [entries[0] + entries[1], entries[0] - entries[1]]
    even, odd = [None] * (n // 4 + 1), [None] * (n // 4 + 1)
    even[0], odd[0] = entries[0] + entries[n // 2], entries[0] - entries[n // 2]
    for k in range(1, n // 4):
        other = entries[n // 2 - k]
        other = (other[0], -other[1])
        even[k] = add(entries[k], other)
        odd[k] = rotate(sub(entries[k], other), k / n)
    middle = entries[n // 4]
    even[n // 4], odd[n // 4] = 2.0 * middle[0], -2.0 * middle[1]
    out = [None] * n
    out[0::2], out[1::2] = real_inverse(even), real_inverse(odd)
    return out


def circulant_tables():
    frequency = np.arange(SIDE)
    wavenumber = np.minimum(frequency, SIDE - frequency).astype(np.float64)
    screening = SIDE / 16.0
    values = screening / np.sqrt(
        wavenumber[:, None] ** 2 + wavenumber[None, :] ** 2 + screening * screening
    )
    values[0, 0] = 0.0
    cosines = np.cos(2 * np.pi * np.outer(frequency, frequency) / SIDE)
    taps = values[: SIDE // 2 + 1] @ cosines / (SIDE * SIDE)
    shift = (frequency[None, :] - frequency[:, None]) % SIDE
    tables = taps[:, shift].astype(np.float32)
    high = tables.astype(jnp.bfloat16)
    low = (tables - high.astype(np.float32)).astype(jnp.bfloat16)
    return jnp.asarray(np.concatenate([high, low], axis=2))


def fetches(step, slot, apart, arrays, cells_ref, in_sem):
    _, column, parts = step[2][apart]
    width = step[1] * SIDE
    return [
        pltpu.make_async_copy(
            arrays[which].at[:, pl.ds(column, width)],
            cells_ref.at[slot, apart, pl.ds(first, size), pl.ds(0, width)],
            in_sem.at[slot, apart],
        )
        for which, first, size in parts
    ]


def holder(step, apart):
    even_mask, odd_mask = step[2][apart][0]
    me, odd = lax.axis_index("grid"), lax.axis_index("pts") & 1
    if even_mask == odd_mask:
        return me ^ even_mask
    return me ^ (even_mask ^ (odd * (even_mask ^ odd_mask)))


def pick_from(step, apart, index_ref, cells):
    width, count = step[1] * SIDE, len(step[2])
    base = holder(step, apart) * (SIDE * SIDE // count) + step[0] * SIDE
    shape = (index_ref.shape[0], width)
    hot = lax.broadcasted_iota(jnp.int32, shape, 1) == index_ref[...] - base
    return lax.dot_general(
        jnp.where(hot, 1.0, 0.0).astype(jnp.bfloat16),
        cells,
        (((1,), (1,)), ((), ())),
        preferred_element_type=jnp.float32,
    )


def pick_kernel(steps, index_ref, *refs):
    *arrays, out_ref, cells_ref, total_ref, in_sem = refs
    count = len(steps[0][2])

    def start(at):
        for apart in range(count):
            for copy in fetches(steps[at], at % 2, apart, arrays, cells_ref, in_sem):
                copy.start()

    start(0)
    total_ref[...] = jnp.zeros_like(total_ref)
    for at, step in enumerate(steps):
        if at + 1 < len(steps):
            start(at + 1)
        for apart in range(count):
            for copy in fetches(step, at % 2, apart, arrays, cells_ref, in_sem):
                copy.wait()
            cells = cells_ref[at % 2, apart, :, : step[1] * SIDE]
            total_ref[...] += pick_from(step, apart, index_ref, cells)
    out_ref[...] = total_ref[...].astype(jnp.bfloat16)


def sheet_kernel(steps, pick_first, index_ref, picked_ref, far_tables_ref, *refs):
    *arrays, out_ref, chosen_ref, cells_ref, squared_ref, slots_ref, stage_ref = refs[:-4]
    tables_ref, in_sem, out_sem, table_sem = refs[-4:]
    table_copy = pltpu.make_async_copy(far_tables_ref, tables_ref, table_sem.at[0])
    count = len(steps[0][2])
    rows = SIDE // count
    points = picked_ref.shape[0]
    half = count // 2
    chunk = 8

    def start(at):
        for apart in range(count):
            for copy in fetches(steps[at], at % 2, apart, arrays, cells_ref, in_sem):
                copy.start()

    def wait(at, apart):
        for copy in fetches(steps[at], at % 2, apart, arrays, cells_ref, in_sem):
            copy.wait()

    for at in range(max(1, pick_first)):
        start(at)
    table_copy.start()
    if pick_first:
        total = picked_ref[...].astype(jnp.float32)
        for at in range(pick_first):
            for apart in range(count):
                wait(at, apart)
                cells = cells_ref[at, apart, :, : steps[at][1] * SIDE]
                total += pick_from(steps[at], apart, index_ref, cells)
        chosen_ref[...] = total.astype(jnp.bfloat16)
    else:
        chosen_ref[...] = picked_ref[...]

    for at, step in enumerate(steps):
        first_row, rows_here, _ = step
        width = rows_here * SIDE
        if max(1, pick_first) <= at + 1 < len(steps):
            start(at + 1)
        for apart in range(count):
            if at >= pick_first:
                wait(at, apart)
            pair = jnp.dot(
                chosen_ref[...],
                cells_ref[at % 2, apart, :, :width],
                preferred_element_type=jnp.float32,
            )
            squared_ref[holder(step, apart), :, :width] = pair * pair

        def spread(here, first_row=first_row, rows_here=rows_here):
            for within in range(rows_here):
                j = first_row + within
                lanes = pl.ds(within * SIDE, SIDE)
                entries = real_dft([squared_ref[g, here, lanes] for g in range(count)])
                slots_ref[0, j, here, :] = entries[0]
                slots_ref[count - 1, j, here, :] = entries[half]
                for k in range(1, half):
                    re, im = rotate(entries[k], -k * j / SIDE)
                    slots_ref[2 * k - 1, j, here, :] = re
                    slots_ref[2 * k, j, here, :] = im

        def one(at_chunk, carry):
            spread(pl.ds(pl.multiple_of(at_chunk * chunk, chunk), chunk))
            return carry

        lax.fori_loop(0, points // chunk, one, 0, unroll=min(2, points // chunk))

    table_copy.wait()

    def circulant(blocks, a):
        stacked = blocks[0] if len(blocks) == 1 else jnp.concatenate(blocks, axis=0)
        high = stacked.astype(jnp.bfloat16)
        low = (stacked - high.astype(jnp.float32)).astype(jnp.bfloat16)
        table = tables_ref[min(a, SIDE - a)]
        both = jnp.dot(
            jnp.concatenate([high, low], axis=1),
            jnp.concatenate([table, table], axis=0),
            preferred_element_type=jnp.float32,
        )
        return both[:, :SIDE] + both[:, SIDE:]

    def over_points(body, unroll):
        def one(at, carry):
            body(pl.ds(pl.multiple_of(at * chunk, chunk), chunk))
            return carry

        lax.fori_loop(0, points // chunk, one, 0, unroll=min(unroll, points // chunk))

    def apply(places, a):
        outs = circulant([slots_ref[s, j, :points, :] for s, j in places], a)
        for at, (s, j) in enumerate(places):
            slots_ref[s, j, :points, :] = outs[at * points : (at + 1) * points]

    def real_there(here):
        entries = real_dft([slots_ref[0, j, here, :] for j in range(rows)])
        slots_ref[0, 0, here, :] = entries[0]
        slots_ref[0, rows - 1, here, :] = entries[rows // 2]
        for k in range(1, rows // 2):
            slots_ref[0, 2 * k - 1, here, :], slots_ref[0, 2 * k, here, :] = entries[k]

    def real_back(here):
        entries = [slots_ref[0, 0, here, :]]
        for k in range(1, rows // 2):
            entries.append((slots_ref[0, 2 * k - 1, here, :], slots_ref[0, 2 * k, here, :]))
        entries.append(slots_ref[0, rows - 1, here, :])
        for j, value in enumerate(real_inverse(entries)):
            slots_ref[0, j, here, :] = value

    over_points(real_there, 4)
    apply([(0, 0)], 0)
    apply([(0, rows - 1)], SIDE // 2)
    for k in range(1, rows // 2):
        apply([(0, 2 * k - 1), (0, 2 * k)], count * k)
    over_points(real_back, 4)

    last = count - 1
    short = rows // 2

    def odd_there(here):
        values = [
            rotate((slots_ref[last, j, here, :], -slots_ref[last, j + short, here, :]), -j / (2 * rows))
            for j in range(short)
        ]
        for k, (re, im) in enumerate(complex_dft(values, -1)):
            slots_ref[last, 2 * k, here, :] = re
            slots_ref[last, 2 * k + 1, here, :] = im

    def odd_back(here):
        values = [
            (slots_ref[last, 2 * k, here, :], slots_ref[last, 2 * k + 1, here, :])
            for k in range(short)
        ]
        for j, value in enumerate(complex_dft(values, 1)):
            re, im = rotate(value, j / (2 * rows))
            slots_ref[last, j, here, :] = 2.0 * re
            slots_ref[last, j + short, here, :] = -2.0 * im

    over_points(odd_there, 4)
    for k in range(short):
        apply([(last, 2 * k), (last, 2 * k + 1)], half + 2 * count * k)
    over_points(odd_back, 4)

    for k in range(1, half):
        re_slot, im_slot = 2 * k - 1, 2 * k

        def complex_there(here, sign=-1):
            values = [
                (slots_ref[re_slot, j, here, :], slots_ref[im_slot, j, here, :])
                for j in range(rows)
            ]
            for j, (re, im) in enumerate(complex_dft(values, sign)):
                slots_ref[re_slot, j, here, :] = re
                slots_ref[im_slot, j, here, :] = im

        over_points(complex_there, 4)
        for a2 in range(rows):
            apply([(re_slot, a2), (im_slot, a2)], k + count * a2)
        over_points(functools.partial(complex_there, sign=1), 4)

    def put(j, slot):
        return [
            pltpu.make_async_copy(
                stage_ref.at[slot, g], out_ref.at[:, rows * g + j, :], out_sem.at[slot]
            )
            for g in range(count)
        ]

    for j in range(rows):
        slot = j % STAGES
        if j >= STAGES:
            for copy in put(j - STAGES, slot):
                copy.wait()

        def gather_back(here):
            entries = [slots_ref[0, j, here, :]]
            for k in range(1, half):
                entries.append(
                    rotate(
                        (slots_ref[2 * k - 1, j, here, :], slots_ref[2 * k, j, here, :]),
                        k * j / SIDE,
                    )
                )
            entries.append(slots_ref[count - 1, j, here, :])
            for g, value in enumerate(real_inverse(entries)):
                stage_ref[slot, g, here, :] = value

        over_points(gather_back, 4)
        for copy in put(j, slot):
            copy.start()
    for j in range(max(rows - STAGES, 0), rows):
        for copy in put(j, j % STAGES):
            copy.wait()


VMEM_SPEC = pl.BlockSpec(memory_space=pltpu.VMEM)
ANY_SPEC = pl.BlockSpec(memory_space=pl.ANY)


def flatten(steps):
    arrays, plan = [], []
    for first_row, rows_here, entries in steps:
        numbered = []
        for masks, column, parts in entries:
            for array, _ in parts:
                if not any(array is known for known in arrays):
                    arrays.append(array)
            which = [next(i for i, known in enumerate(arrays) if known is array) for array, _ in parts]
            numbered.append(
                (masks, column, tuple((w, first, a.shape[0]) for w, (a, first) in zip(which, parts)))
            )
        plan.append((first_row, rows_here, tuple(numbered)))
    return tuple(plan), arrays


def cell_buffers(plan, orbital_count):
    widest = max(rows_here for _, rows_here, _ in plan) * SIDE
    return pltpu.VMEM((min(2, len(plan)), len(plan[0][2]), orbital_count, widest), jnp.bfloat16)


def pick_cells(index, orbital_count, steps, us=0):
    plan, arrays = flatten(steps)
    count = len(plan[0][2])
    shape = (index.shape[0], orbital_count)
    return pl.pallas_call(
        functools.partial(pick_kernel, plan),
        in_specs=[VMEM_SPEC] + [ANY_SPEC] * len(arrays),
        out_specs=VMEM_SPEC,
        out_shape=jax.ShapeDtypeStruct(shape, jnp.bfloat16),
        scratch_shapes=[
            cell_buffers(plan, orbital_count),
            pltpu.VMEM(shape, jnp.float32),
            pltpu.SemaphoreType.DMA((2, count)),
        ],
        compiler_params=pltpu.CompilerParams(vmem_limit_bytes=VMEM_BYTES),
        cost_estimate=pl.CostEstimate(flops=us * 5 * 10**8, bytes_accessed=0, transcendentals=0),
    )(index, *arrays)


def screen_sheets(index, picked, tables, steps, pick_first):
    points, orbital_count = picked.shape
    plan, arrays = flatten(steps)
    count = len(plan[0][2])
    rows = SIDE // count
    widest = max(rows_here for _, rows_here, _ in plan) * SIDE
    return pl.pallas_call(
        functools.partial(sheet_kernel, plan, pick_first),
        in_specs=[VMEM_SPEC] * 2 + [ANY_SPEC] * (1 + len(arrays)),
        out_specs=ANY_SPEC,
        out_shape=jax.ShapeDtypeStruct((points, SIDE, SIDE), jnp.float32),
        scratch_shapes=[
            pltpu.VMEM((points, orbital_count), jnp.bfloat16),
            cell_buffers(plan, orbital_count),
            pltpu.VMEM((count, points, widest), jnp.float32),
            pltpu.VMEM((count, rows, points + 8, SIDE), jnp.float32),
            pltpu.VMEM((STAGES, count, points, SIDE), jnp.float32),
            pltpu.VMEM(tables.shape, tables.dtype),
            pltpu.SemaphoreType.DMA((2, count)),
            pltpu.SemaphoreType.DMA((STAGES,)),
            pltpu.SemaphoreType.DMA((1,)),
        ],
        compiler_params=pltpu.CompilerParams(vmem_limit_bytes=VMEM_BYTES),
    )(index, picked, tables, *arrays)


def swap(array, mask):
    count = lax.axis_size("grid")
    return lax.ppermute(array, "grid", [(i, i ^ mask) for i in range(count)])


def routes(bits):
    cut = (bits - 1) // 2
    links = list(range(1, bits))
    return links, links[cut:] + links[:cut]


class Order:
    def __init__(self, seed):
        self.token = seed

    def start(self, move, array, *arguments):
        array, _ = lax.optimization_barrier((array, self.token))
        return move(array, *arguments)

    def wait(self, *arrays):
        self.token, *_ = lax.optimization_barrier((self.token, *arrays))


def gather_cells(orbitals):
    count = lax.axis_size("grid")
    bits = count.bit_length() - 1
    middle = orbitals.shape[0] // 2
    held = {0: [(orbitals, 0)]}
    pieces = ({0: orbitals[:middle]}, {0: orbitals[middle:]})
    for route, have in zip(routes(bits), pieces):
        for bit in route:
            for known in sorted(have):
                have[known | 1 << bit] = swap(have[known], 1 << bit)
    for known in pieces[0]:
        if known:
            held[known] = [(pieces[0][known], 0), (pieces[1][known], middle)]
    for known in sorted(held):
        held[known | 1] = [(swap(array, 1), first) for array, first in held[known]]
    rows = SIDE // count
    return [
        (j, 1, [((d, d), j * SIDE, held[d]) for d in range(count)]) for j in range(rows)
    ]


CORE, NEAR, FAR = 1, 2, 4
SCRIPT = ("F0", "F1", "B", "P0", "F2", "P1", "F3", "S0", "P2", "W", "S1", "X3", "V2", "P3", "S2", "K012:0", "S3")
PIECE_ROWS = (4, 4, 4, 4)


def exchange(array, masks, across):
    count, planes = lax.axis_size("grid"), lax.axis_size("pts")
    pairs = [
        (g * planes + z, (g ^ masks[z & 1]) * planes + (z ^ across))
        for g in range(count)
        for z in range(planes)
    ]
    return lax.ppermute(array, ("grid", "pts"), pairs)


def four_chips(orbitals, index, seed, tables):
    order = Order(seed)
    ends = [sum(PIECE_ROWS[:p]) for p in range(len(PIECE_ROWS) + 1)]
    first, far, core = {}, {}, {}

    def send_first(p):
        source = lax.optimization_barrier((orbitals, order.token))[0]
        piece = source[:, ends[p] * SIDE : ends[p + 1] * SIDE]
        first[p] = exchange(piece, (NEAR, FAR), 0)

    def pass_on(p):
        order.wait(first[p])
        far[p] = (
            order.start(exchange, first[p], (FAR, NEAR), 0),
            order.start(exchange, first[p], (0, 0), 1),
        )
        core[p] = [order.start(swap, first[p], CORE)]

    def share(p):
        if p < len(PIECE_ROWS) - 1:
            order.wait(*far[p])
        for array in far[p]:
            order.wait(array)
            core[p].append(order.start(swap, array, CORE))

    def step(p):
        order.wait(*core[p])
        entry = [
            ((0, 0), ends[p] * SIDE, [(orbitals, 0)]),
            ((CORE, CORE), ends[p] * SIDE, [(sibling, 0)]),
        ]
        arrays = (first[p], *far[p])
        for masks, array, other in zip(((NEAR, FAR), (NEAR | FAR,) * 2, (FAR, NEAR)), arrays, core[p]):
            entry.append((masks, 0, [(array, 0)]))
            entry.append((tuple(m | CORE for m in masks), 0, [(other, 0)]))
        return (ends[p], PIECE_ROWS[p], entry)

    steps, picks = {}, []
    for word in SCRIPT:
        op, arg = word[0], word[1:]
        if op == "F":
            send_first(int(arg))
        elif op == "P":
            pass_on(int(arg))
        elif op == "S":
            share(int(arg))
        elif op == "V":
            order.wait(*far[int(arg)])
        elif op == "X":
            order.wait(first[int(arg)])
        elif op == "B":
            sibling = order.start(swap, orbitals, CORE)
        elif op == "W":
            order.wait(sibling)
        elif op == "K":
            ids, cost = arg.split(":")
            for p in ids:
                steps[int(p)] = step(int(p))
            picks.append(pick_cells(index, orbitals.shape[0], [steps[int(p)] for p in ids], int(cost)))
            order.wait(picks[-1])
    left = [step(p) for p in range(len(PIECE_ROWS)) if p not in steps]
    picked = functools.reduce(lambda x, y: x + y, picks)
    return screen_sheets(index, picked, tables, left + [steps[p] for p in sorted(steps)], len(left))


def shards(orbitals, point_index):
    count = lax.axis_size("grid")
    points = point_index.shape[0] // count
    index = lax.dynamic_slice_in_dim(point_index, lax.axis_index("grid") * points, points)[:, None]
    tables = circulant_tables()
    if count == 8 and lax.axis_size("pts") % 2 == 0:
        return four_chips(orbitals, index, point_index[:1], tables)[None]
    steps = gather_cells(orbitals)
    picked = pick_cells(index, orbitals.shape[0], steps)
    return screen_sheets(index, picked, tables, steps, 0)[None]


def solution(mesh):
    in_specs = (P(None, "grid"), P("pts"))
    out_specs = P("pts", "grid", None, None)
    return jax.shard_map(shards, mesh=mesh, in_specs=in_specs, out_specs=out_specs, check_vma=False)
```
